32 devices in a mesh: groups: 2 (over y), seq: 4 (over z), exp: 4 (over x, core).
Axes of the slice: x: 2, y: 2, z: 4, core: 2. Of those that a mesh axis runs over, the one named last changes fastest.
Arguments:
- residual: bfloat16 [1024, 6144], P(('groups', 'seq'), 'exp'), parts along dimension 0, may hold values from -6 to 6
- query_rows: bfloat16 [1024, 6144], P(('groups', 'seq'), 'exp'), parts along dimension 0, may hold values from -6 to 6
- key_rows: bfloat16 [1024, 6144], P(('groups', 'seq'), 'exp'), parts along dimension 0, may hold values from -6 to 6
- value_rows: bfloat16 [1024, 6144], P(('groups', 'seq'), 'exp'), parts along dimension 0, may hold values from -6 to 6
- log_decay: float32 [1024, 48], P(('groups', 'seq'), 'exp'), parts along dimension 0, may hold values from -0.8 to 0
- attn_gain: float32 [6144], P('exp'), may hold values from 0.1 to 1.9
- norm_gain: float32 [6144], P('exp'), may hold values from 0.1 to 1.9
- router: bfloat16 [6144, 32], P('exp'), may hold values from -0.3125 to 0.3125
- expert_ids: int32 [1024, 2], P(('groups', 'seq')), parts along dimension 0, may hold values from 0 to 31, all different within a row
- priority: int32 [8, 128], P(('groups', 'seq')), parts along dimension 0, may hold values from 0 to 127, each once within a row
- gate_weight: bfloat16 [4, 6144, 4608], P('exp', None, 'seq'), may hold values from -0.078125 to 0.078125
- up_weight: bfloat16 [4, 6144, 4608], P('exp', None, 'seq'), may hold values from -0.078125 to 0.078125
- down_weight: bfloat16 [4, 4608, 6144], P('exp', None, 'seq'), may hold values from -0.125 to 0.125
Outputs:
- layer_out: bfloat16 [1024, 6144], P(('groups', 'seq'), 'exp'), parts along dimension 0
The draws below stay inside these ranges and needn't reach their ends.
There are 2 independent parts, one for each index of `groups`. The reference program is written for one: setup_inputs(seed, part) draws one part's arguments, and reference() takes and returns one part's arrays. A program takes and returns all parts, laid end to end along the dimension named above; an argument that names none is the same for every part. Nothing has to cross between parts.
Inputs may be any that keep to these rules, and one draw needn't show every extreme that they name: `expert_ids`: each row names two different experts; ids of 4 or more name experts whose weights are not given. `priority`: each row holds every number from 0 to 127 once.
All inputs are finite; a program needn't handle non-finite values.
Results may differ from the reference program's by a relative error of at most 0.0047.
Values may be sent and summed in bfloat16 or wider, within the bound.
A program may use at most 128 MiB of HBM per device.

```python
import math
import jax
import jax.numpy as jnp
from jax import lax

D = 6144
HEAD = 128
HEADS = 48
FF = 4608
EXPERTS = 32
TOP = 2
TOK_DEV = 128
TOKENS = 512
HELD = 4
CAP = 8
N_SEQ = 4


def draw_log_decay(key, part):
    streams = jax.random.split(jax.random.fold_in(key, 17), 5)
    share = 0.5
    fast = jax.random.uniform(streams[0], (HEADS,)) < share
    rough = jnp.exp(jax.random.uniform(streams[1], (TOKENS, HEADS), minval=-0.69, maxval=0.69))
    blocks = TOKENS // TOK_DEV
    blockwise = jnp.exp(jax.random.uniform(streams[2], (blocks, 1, HEADS), minval=-0.69, maxval=0.69))
    blockwise = jnp.broadcast_to(blockwise, (blocks, TOK_DEV, HEADS)).reshape(TOKENS, HEADS)
    slow_rate = 0.25 * math.log(10.0) / TOKENS
    rate = jnp.where(fast, 1.0 / 40.0, slow_rate)[None, :] * rough * blockwise
    places = jax.random.randint(streams[3], (4,), 0, TOKENS)
    bursty = jnp.any(jnp.arange(TOKENS)[:, None] == places[None, :], axis=1)
    loss = jax.random.uniform(streams[4], (HEADS,), minval=0.2, maxval=0.5)
    jump = jnp.where(bursty[:, None] & jnp.logical_not(fast)[None, :], jnp.log(1.0 - loss)[None, :], 0.0)
    return (jump - rate).astype(jnp.float32)


def raised(array, own_key, source, target, parts, factor):
    def block_of(dim):
        return (jnp.arange(array.shape[dim]) // (array.shape[dim] // parts)).reshape((-1,) + (1,) * (array.ndim - 1 - dim))

    first = jax.random.permutation(own_key, parts)[block_of(target)]
    second = (block_of(target) + parts // 2) % parts
    return jnp.where((block_of(source) == first) | (block_of(source) == second), factor * array, array)


def shard_levels(stream_key, extent, pieces, low, high):
    gain = 1.0
    for axis_at, parts in pieces:
        draws = jax.random.uniform(jax.random.fold_in(jax.random.fold_in(stream_key, 6), axis_at), (parts,), jnp.float32, low / len(pieces), high / len(pieces))
        gain = gain * jnp.repeat(jnp.exp(draws), extent[axis_at] // parts).reshape((-1,) + (1,) * (len(extent) - 1 - axis_at))
    return gain


def choose_distinct(rng, rows, number_of, top, lift):
    ranking = jax.random.permutation(jax.random.fold_in(rng, 1), number_of)
    favour = ranking
    for power in range(3):
        favour = favour * favour // number_of
    favour = favour * lift // number_of
    tickets = jax.random.randint(jax.random.fold_in(rng, 2), (rows, number_of), 0, 4096) + favour
    fixed_rows = jax.random.permutation(jax.random.fold_in(rng, 3), rows)[jnp.arange(number_of) % rows]
    tickets = jnp.where(jnp.arange(rows)[:, None] == fixed_rows[None, :], 1 << 14, tickets)
    score = tickets * number_of + jnp.arange(number_of)
    return lax.top_k(score.astype(jnp.int32), top)[1].astype(jnp.int32)


def gaussian(stream_key, extent, scale, reach, shards=(), kind=jnp.bfloat16):
    array = scale * jax.random.normal(stream_key, extent, jnp.float32)
    if shards:
        array = array * shard_levels(stream_key, extent, shards, -0.22, 0.18)
    return jnp.clip(array, -reach, reach).astype(kind)


def gaussian_with(stream_key, dims, width, bound, cuts, heavy, held_as=jnp.bfloat16):
    array = width * jax.random.normal(stream_key, dims, jnp.float32)
    if cuts:
        array = array * shard_levels(stream_key, dims, cuts, -0.22, 0.18)
    return jnp.clip(raised(array, jax.random.fold_in(stream_key, 3), *heavy), -bound, bound).astype(held_as)


def setup_inputs(seed: int = 0, part: int = 0) -> dict:
    arg_keys = jax.random.split(jax.random.key(seed), 14)
    own_keys = jax.random.split(jax.random.fold_in(arg_keys[13], part), 14)
    return {
        "residual": gaussian(own_keys[0], (TOKENS, D), 1.0, 6.0, ((0, 4), (1, 4))),
        "query_rows": gaussian(own_keys[1], (TOKENS, D), 1.0, 6.0, ((0, 4), (1, 4))),
        "key_rows": gaussian(own_keys[2], (TOKENS, D), 1.0, 6.0, ((0, 4), (1, 4))),
        "value_rows": gaussian(own_keys[3], (TOKENS, D), 1.0, 6.0, ((0, 4), (1, 4))),
        "log_decay": draw_log_decay(jax.random.fold_in(jax.random.fold_in(arg_keys[13], part), 71), part),
        "attn_gain": jnp.clip(1.0 + 0.18 * jax.random.normal(arg_keys[5], (D,), jnp.float32), 0.1, 1.9),
        "norm_gain": jnp.clip(1.0 + 0.18 * jax.random.normal(arg_keys[6], (D,), jnp.float32), 0.1, 1.9),
        "router": gaussian(arg_keys[7], (D, EXPERTS), (D // 16) ** -0.5, 0.3125, ((0, 4),)),
        "expert_ids": choose_distinct(own_keys[8], TOKENS, EXPERTS, TOP, 512),
        "priority": jax.vmap(lambda own: jax.random.permutation(own, TOK_DEV))(jax.random.split(own_keys[9], N_SEQ)).reshape((N_SEQ, TOK_DEV)).astype(jnp.int32),
        "gate_weight": gaussian(arg_keys[10], (HELD, D, FF), D ** -0.5, 0.078125, ((0, 4), (2, 4))),
        "up_weight": gaussian(arg_keys[11], (HELD, D, FF), D ** -0.5, 0.078125, ((0, 4), (2, 4))),
        "down_weight": gaussian_with(arg_keys[12], (HELD, FF, D), FF ** -0.5, 0.125, ((0, 4), (2, 4)), (1, 2, 4, 2.0)),
    }


def block_local(inputs):
    queries, keys, values, cumulative = inputs
    rows = queries.shape[0]
    scores = jnp.einsum('thd,shd->hts', queries.astype(jnp.float32), keys.astype(jnp.float32))
    causal = (jnp.arange(rows)[:, None] >= jnp.arange(rows)[None, :])[None]
    spread = cumulative.T[:, :, None] - cumulative.T[:, None, :]
    weights = jnp.where(causal, scores * jnp.exp(jnp.where(causal, spread, 0.0)), 0.0).astype(jnp.bfloat16)
    local_part = jnp.einsum('hts,shd->thd', weights.astype(jnp.float32), values.astype(jnp.float32))
    to_end = jnp.exp(cumulative[-1][None, :] - cumulative)
    keyed = (keys.astype(jnp.float32) * to_end[:, :, None]).astype(jnp.bfloat16)
    state = jnp.einsum('thd,the->hde', keyed.astype(jnp.float32), values.astype(jnp.float32))
    return (local_part, state, jnp.exp(cumulative[-1]))

def reference(residual, query_rows, key_rows, value_rows, log_decay, attn_gain, norm_gain, router, expert_ids, priority, gate_weight, up_weight, down_weight):
    blocks = TOKENS // TOK_DEV
    queries = query_rows.reshape(blocks, TOK_DEV, HEADS, HEAD)
    keys = key_rows.reshape(blocks, TOK_DEV, HEADS, HEAD)
    values = value_rows.reshape(blocks, TOK_DEV, HEADS, HEAD)
    cumulative = jnp.cumsum(log_decay.reshape(blocks, TOK_DEV, HEADS), axis=1)
    local_part, states, decays = lax.map(block_local, (queries, keys, values, cumulative))

    def advance(carry, inputs):
        state, decay = inputs
        return (decay[:, None, None] * carry + state, carry)
    start = jnp.zeros((HEADS, HEAD, HEAD), jnp.float32)
    _, carried = lax.scan(advance, start, (states, decays))
    inter = jnp.einsum('bthd,bhde->bthe', queries.astype(jnp.float32), carried, precision=lax.Precision.HIGHEST)
    attended = local_part + jnp.exp(cumulative)[:, :, :, None] * inter
    normed = attended * lax.rsqrt(lax.optimization_barrier(jnp.mean(attended * attended, axis=-1, keepdims=True)) + 1e-06)
    normed = normed * attn_gain.reshape(HEADS, HEAD)
    mixed = (residual.astype(jnp.float32) + normed.reshape(TOKENS, D)).astype(jnp.bfloat16)
    mixed_f = mixed.astype(jnp.float32)
    inverse = lax.rsqrt(lax.optimization_barrier(jnp.sum(mixed_f * mixed_f, axis=1)) / D + 1e-06)
    scaled = mixed_f * norm_gain * inverse[:, None]
    tokens_in = scaled.astype(jnp.bfloat16)
    logits = jnp.dot(scaled, router.astype(jnp.float32), precision=lax.Precision.HIGHEST)
    probs = jax.nn.sigmoid(logits)
    chosen = expert_ids[:, :, None] == jnp.arange(EXPERTS, dtype=jnp.int32)[None, None, :]
    selected = lax.optimization_barrier(jnp.sum(jnp.where(chosen, probs[:, None, :], 0.0), axis=-1))
    gates = selected / lax.optimization_barrier(jnp.sum(selected, axis=-1, keepdims=True))
    is_held = expert_ids[:, :, None] == jnp.arange(HELD, dtype=jnp.int32)[None, None, :]
    member = jnp.where(jnp.any(is_held, axis=1), 1.0, 0.0).astype(jnp.float32)
    gate_held = lax.optimization_barrier(jnp.sum(jnp.where(is_held, gates[:, :, None], 0.0), axis=1))
    earlier = jnp.where(priority[:, None, :] < priority[:, :, None], 1.0, 0.0).astype(jnp.float32)
    member_b = member.reshape(blocks, TOK_DEV, HELD)
    rank = jnp.einsum('bts,bse->bte', earlier, member_b)
    kept = (member_b > 0.5) & (rank < CAP)
    slot_ids = jnp.arange(CAP).astype(rank.dtype)
    place = kept.transpose(0, 2, 1)[:, :, None, :] & (rank.transpose(0, 2, 1)[:, :, None, :] == slot_ids[None, None, :, None])
    place_f = jnp.where(place, 1.0, 0.0).astype(jnp.float32)
    buffers = jnp.einsum('bect,btd->ebcd', place_f, tokens_in.reshape(blocks, TOK_DEV, D).astype(jnp.float32)).astype(jnp.bfloat16)

    def run_expert(inputs):
        slots, gate_w, up_w, down_w = inputs
        rows = slots.reshape(blocks * CAP, D)
        gate = jnp.dot(rows, gate_w, preferred_element_type=jnp.float32)
        up = jnp.dot(rows, up_w, preferred_element_type=jnp.float32)
        hidden = (jax.nn.silu(gate) * up).astype(jnp.bfloat16)
        return jnp.dot(hidden, down_w, preferred_element_type=jnp.float32).astype(jnp.bfloat16)
    expert_out = lax.map(run_expert, (buffers, gate_weight, up_weight, down_weight))
    expert_out = expert_out.reshape(HELD, blocks, CAP, D).astype(jnp.float32)
    weighted = place_f * gate_held.reshape(blocks, TOK_DEV, HELD).transpose(0, 2, 1)[:, :, None, :]
    combined = jnp.einsum('bect,ebcd->btd', weighted, expert_out, precision=lax.Precision.HIGHEST)
    return (mixed_f + combined.reshape(TOKENS, D)).astype(jnp.bfloat16)
```

```python
import functools

import jax
import jax.numpy as jnp
from jax import lax
from jax.experimental import pallas as pl
from jax.experimental.pallas import tpu as pltpu
from jax.sharding import PartitionSpec as P

D = 6144
HEAD = 128
EXPERTS = 32
CAP = 8


def link_states(earlier, later):
    return (earlier[0] * later[0], later[0] * earlier[1] + later[1])


def plain_body(
    residual,
    query_rows,
    key_rows,
    value_rows,
    log_decay,
    attn_gain,
    norm_gain,
    router,
    expert_ids,
    priority,
    gate_weight,
    up_weight,
    down_weight,
):
    rows = residual.shape[0]
    width = residual.shape[1]
    heads = width // HEAD
    held = lax.axis_size("exp")
    queries = query_rows.reshape(rows, heads, HEAD)
    keys_local = key_rows.reshape(rows, heads, HEAD)
    values = value_rows.reshape(rows, heads, HEAD)
    cumulative = jnp.cumsum(log_decay, axis=0)
    scores = jnp.einsum("thd,shd->hts", queries, keys_local, preferred_element_type=jnp.float32)
    causal = (jnp.arange(rows)[:, None] >= jnp.arange(rows)[None, :])[None]
    spread = cumulative.T[:, :, None] - cumulative.T[:, None, :]
    weights = jnp.where(causal, scores * jnp.exp(jnp.where(causal, spread, 0.0)), 0.0).astype(
        jnp.bfloat16
    )
    local_part = jnp.einsum("hts,shd->thd", weights, values, preferred_element_type=jnp.float32)
    to_end = jnp.exp(cumulative[-1][None, :] - cumulative)
    keyed = (keys_local.astype(jnp.float32) * to_end[:, :, None]).astype(jnp.bfloat16)
    block_state = jnp.einsum("thd,the->hde", keyed, values, preferred_element_type=jnp.float32)
    block_decay = jnp.exp(cumulative[-1])
    seq_count = lax.axis_size("seq")
    share_size = block_state.size // seq_count
    flat_state = block_state.reshape(seq_count, share_size)
    tiled_decay = jnp.broadcast_to(block_decay[None, :], (seq_count, heads))
    arrived_state, arrived_decay = (
        lax.all_to_all(flat_state, "seq", split_axis=0, concat_axis=0, tiled=True),
        lax.all_to_all(tiled_decay, "seq", split_axis=0, concat_axis=0, tiled=True),
    )
    position = lax.axis_index("seq") * share_size + jnp.arange(share_size, dtype=jnp.int32)
    owner_head = position // (HEAD * HEAD)
    selector = jnp.where(
        owner_head[None, :] == jnp.arange(heads, dtype=jnp.int32)[:, None], 1.0, 0.0
    ).astype(jnp.float32)
    element_decay = jnp.dot(arrived_decay, selector, precision=lax.Precision.HIGHEST)
    inclusive = lax.associative_scan(link_states, (element_decay, arrived_state), axis=0)[1]
    exclusive = jnp.concatenate([jnp.zeros((1, share_size), jnp.float32), inclusive[:-1]], axis=0)
    returned_prefix = lax.all_to_all(exclusive, "seq", split_axis=0, concat_axis=0, tiled=True)
    prior_state = returned_prefix.reshape(block_state.shape)
    inter = jnp.einsum(
        "thd,hde->the", queries.astype(jnp.float32), prior_state, precision=lax.Precision.HIGHEST
    )
    attended = local_part + jnp.exp(cumulative)[:, :, None] * inter
    normed = attended * lax.rsqrt(jnp.mean(attended * attended, axis=-1, keepdims=True) + 1e-06)
    normed = normed * attn_gain.reshape(heads, HEAD)
    mixed = (residual.astype(jnp.float32) + normed.reshape(rows, width)).astype(jnp.bfloat16)
    mixed_f = mixed.astype(jnp.float32)
    gained = mixed_f * norm_gain
    router_f = router.astype(jnp.float32)
    squares = lax.psum(jnp.sum(mixed_f * mixed_f, axis=1), "exp")
    inverse = lax.rsqrt(squares / D + 1e-06)
    scaled = gained * inverse[:, None]
    logits = lax.psum(jnp.dot(scaled, router_f, precision=lax.Precision.HIGHEST), "exp")
    tokens_in = scaled.astype(jnp.bfloat16)
    probs = jax.nn.sigmoid(logits)
    chosen = expert_ids[:, :, None] == jnp.arange(EXPERTS, dtype=jnp.int32)[None, None, :]
    selected = jnp.sum(jnp.where(chosen, probs[:, None, :], 0.0), axis=-1)
    gates = selected / jnp.sum(selected, axis=-1, keepdims=True)
    is_held = expert_ids[:, :, None] == jnp.arange(held, dtype=jnp.int32)[None, None, :]
    member = jnp.where(jnp.any(is_held, axis=1), 1.0, 0.0).astype(jnp.float32)
    gate_held = jnp.sum(jnp.where(is_held, gates[:, :, None], 0.0), axis=1)
    order = priority[0]
    earlier = jnp.where(order[None, :] < order[:, None], 1.0, 0.0).astype(jnp.bfloat16)
    rank = jnp.dot(earlier, member.astype(jnp.bfloat16), preferred_element_type=jnp.float32)
    kept = (member > 0.5) & (rank < CAP)
    slot_ids = jnp.arange(CAP).astype(jnp.float32)
    place = kept.T[:, None, :] & (rank.T[:, None, :] == slot_ids[None, :, None])
    place_f = jnp.where(place, 1.0, 0.0).astype(jnp.float32)
    buffer = jnp.einsum(
        "ect,td->ecd", place_f.astype(jnp.bfloat16), tokens_in, preferred_element_type=jnp.float32
    ).astype(jnp.bfloat16)
    arrived = lax.all_to_all(buffer, "exp", split_axis=0, concat_axis=2, tiled=True)[0]
    gathered = lax.all_gather(arrived, "seq", axis=0, tiled=True)
    gate = jnp.dot(gathered, gate_weight[0], preferred_element_type=jnp.float32)
    up = jnp.dot(gathered, up_weight[0], preferred_element_type=jnp.float32)
    hidden = (jax.nn.silu(gate) * up).astype(jnp.bfloat16)
    weight_rows = down_weight[0]
    summed = jnp.dot(
        lax.all_gather(hidden, "seq", axis=1, tiled=True),
        weight_rows,
        preferred_element_type=jnp.float32,
    )
    expert_out = summed.astype(jnp.bfloat16)
    returned = lax.all_to_all(expert_out, "seq", split_axis=0, concat_axis=1, tiled=True)
    regrouped = lax.all_to_all(returned[None], "exp", split_axis=2, concat_axis=0, tiled=True)
    weighted = place_f * gate_held.T[:, None, :]
    combined = jnp.einsum(
        "ect,ecd->td", weighted, regrouped.astype(jnp.float32), precision=lax.Precision.HIGHEST
    )
    return (mixed_f + combined).astype(jnp.bfloat16)


MESH = pl.DeviceIdType.MESH
F32 = jnp.float32
BF16 = jnp.bfloat16
WEIGHT_CUTS = 4


def layer_kernel(
    ns,
    nx,
    group,
    residual,
    query,
    key,
    value,
    log_decay,
    attn_gain,
    norm_gain,
    router,
    ids,
    priority,
    gate_hbm,
    up_hbm,
    down_hbm,
    out,
    weights_in,
    weights_down,
    padded,
    cum_rows,
    mixed,
    chain_out,
    chain_in,
    sums_out,
    sums_in,
    slots_out,
    slots_in,
    inverse_out,
    inverse_in,
    total_in,
    hidden_all,
    total_out,
    back_out,
    back_in,
    weight_sems,
    chain_sems,
    sums_send,
    sums_recv,
    slots_send,
    slots_recv,
    inverse_send,
    inverse_recv,
    hidden_send,
    hidden_recv,
    back_send,
    back_recv,
):
    rows, width = residual.shape
    heads = width // HEAD
    half = width // 2
    depth = weights_in.shape[0]
    ff = gate_hbm.shape[2]
    s = lax.axis_index("seq")
    x = lax.axis_index("exp")

    weight_copies = []
    cut = depth // WEIGHT_CUTS
    for i in range(WEIGHT_CUTS):
        at = pl.ds(i * cut, cut)
        weight_copies.append(
            pltpu.make_async_copy(
                gate_hbm.at[0, at, :], weights_in.at[at, pl.ds(0, ff)], weight_sems.at[0, i]
            )
        )
        weight_copies.append(
            pltpu.make_async_copy(
                up_hbm.at[0, at, :], weights_in.at[at, pl.ds(ff, ff)], weight_sems.at[1, i]
            )
        )
    down_copies = []
    cut = weights_down.shape[0] // WEIGHT_CUTS
    for i in range(WEIGHT_CUTS):
        at = pl.ds(i * cut, cut)
        down_copies.append(
            pltpu.make_async_copy(down_hbm.at[0, at, :], weights_down.at[at, :], weight_sems.at[2, i])
        )
    for copy in weight_copies + down_copies:
        copy.start()

    barrier = pltpu.get_barrier_semaphore()
    peers = [(a, b) for a in range(ns) for b in range(nx) if (a, b) != (0, 0)]

    def peer(a, b):
        return {"seq": lax.rem(s + a, ns), "exp": lax.rem(x + b, nx)}

    for a, b in peers:
        pl.semaphore_signal(barrier, inc=1, device_id=peer(a, b), device_id_type=MESH)

    row_at = lax.broadcasted_iota(jnp.int32, (rows, rows), 0)
    lane_at = lax.broadcasted_iota(jnp.int32, (rows, rows), 1)
    id_cols = [ids[:, i : i + 1] for i in range(2)]
    ids_t = jnp.where(
        lane_at == 0,
        id_cols[0].astype(F32),
        jnp.where(lane_at == 1, id_cols[1].astype(F32), 0.0),
    ).T
    id_rows = [ids_t[i : i + 1, :] for i in range(2)]
    order = jnp.broadcast_to(priority[...].astype(F32), (rows, rows))
    earlier = jnp.where(order.T < order, 1.0, 0.0).astype(BF16)
    expert_rows = -(-nx // 8) * 8
    expert_at = lax.broadcasted_iota(jnp.int32, (expert_rows, rows), 0).astype(F32)
    member = jnp.where((id_rows[0] == expert_at) | (id_rows[1] == expert_at), 1.0, 0.0)
    rank = jnp.dot(member.astype(BF16), earlier, preferred_element_type=F32)
    slot_at = lax.broadcasted_iota(jnp.int32, (CAP, rows), 0).astype(F32)
    rank = jnp.where(member > 0.5, rank, -1.0)
    place = [jnp.where(rank[e : e + 1, :] == slot_at, 1.0, 0.0) for e in range(nx)]
    place_all = jnp.concatenate(place, axis=0)

    padded[...] = jnp.zeros_like(padded)
    padded[:, :heads] = log_decay[...]
    lower = jnp.where(row_at >= lane_at, 1.0, 0.0).astype(F32)
    cumulative = jnp.dot(
        lower, padded[...], precision=lax.Precision.HIGHEST, preferred_element_type=F32
    )
    padded[...] = cumulative
    cum_rows[...] = cumulative.T

    @pl.when(s == 0)
    def _():
        chain_in[...] = jnp.zeros_like(chain_in)

    pl.semaphore_wait(barrier, len(peers))

    def chain_copy(i):
        return pltpu.make_async_remote_copy(
            src_ref=chain_out.at[i],
            dst_ref=chain_in.at[i],
            send_sem=chain_sems.at[0, i],
            recv_sem=chain_sems.at[1, i],
            device_id={"seq": lax.rem(s + 1, ns)},
            device_id_type=MESH,
        )

    causal = row_at >= lane_at

    def attend(i, carry):
        held = []
        for g in range(group):
            head = i * group + g
            at = pl.ds(pl.multiple_of(head * HEAD, HEAD), HEAD)
            col = jnp.sum(jnp.where(lane_at == head, padded[...], 0.0), axis=1, keepdims=True)
            row = cum_rows[pl.ds(head, 1), :]
            last = col[rows - 1 : rows, :]
            q, k, v = query[:, at], key[:, at], value[:, at]
            keyed = (k.astype(F32) * jnp.exp(last - col)).astype(BF16)
            state = lax.dot_general(
                keyed, v, (((0,), (0,)), ((), ())), preferred_element_type=F32
            )
            scores = lax.dot_general(q, k, (((1,), (1,)), ((), ())), preferred_element_type=F32)
            spread = jnp.where(causal, col - row, 0.0)
            weights = jnp.where(causal, scores * jnp.exp(spread), 0.0).astype(BF16)
            local = jnp.dot(weights, v, preferred_element_type=F32)
            held.append((at, q, state, jnp.exp(last), local, jnp.exp(col)))

        @pl.when(s > 0)
        def _():
            chain_copy(i).wait_recv()

        @pl.when(s < ns - 1)
        def _():
            for g in range(group):
                prior = chain_in[i, g].astype(F32)
                chain_out[i, g] = (held[g][3] * prior + held[g][2]).astype(BF16)
            chain_copy(i).start()

        for g in range(group):
            at, q, _, _, local, grown = held[g]
            inter = jnp.dot(q, chain_in[i, g], preferred_element_type=F32)
            attended = local + grown * inter
            mean = jnp.sum(attended * attended, axis=1, keepdims=True) / HEAD
            normed = attended * lax.rsqrt(mean + 1e-06) * attn_gain[:, at]
            mixed[:, at] = (residual[:, at].astype(F32) + normed).astype(BF16)
        return carry

    lax.fori_loop(0, heads // group, attend, 0)

    mixed_f = mixed[...].astype(F32)
    gained = mixed_f * norm_gain[...]
    tokens = gained.astype(BF16)
    place_b = place_all.astype(BF16)
    for h in range(2):
        part = jnp.dot(
            place_b, tokens[:, h * half : (h + 1) * half], preferred_element_type=F32
        )
        if h == 0:
            first = part
    for e in range(nx):
        at = slice(e * CAP, (e + 1) * CAP)
        slots_out[e] = jnp.concatenate([first[at], part[at]], axis=0).astype(BF16)
    slots_in[s, x] = slots_out[x]

    def slots_copy(a, b):
        return pltpu.make_async_remote_copy(
            src_ref=slots_out.at[lax.rem(x + b, nx)],
            dst_ref=slots_in.at[s, x],
            send_sem=slots_send.at[a, b],
            recv_sem=slots_recv.at[s, x],
            device_id=peer(a, b),
            device_id_type=MESH,
        )

    def slots_arrive(block, source):
        return pltpu.make_async_remote_copy(
            src_ref=slots_out.at[0],
            dst_ref=slots_in.at[block, source],
            send_sem=slots_send.at[0, 0],
            recv_sem=slots_recv.at[block, source],
            device_id=peer(1, 1),
            device_id_type=MESH,
        )

    for a, b in peers:
        slots_copy(a, b).start()

    rest = (gained - tokens.astype(F32)).astype(BF16)
    logits = jnp.dot(tokens, router[...], preferred_element_type=F32) + jnp.dot(
        rest, router[...], preferred_element_type=F32
    )
    expert_lane = lax.broadcasted_iota(jnp.int32, logits.shape, 1)
    picked = [
        jnp.sum(jnp.where(expert_lane == c, logits, 0.0), axis=1, keepdims=True) for c in id_cols
    ]
    squares = jnp.sum(mixed_f * mixed_f, axis=1, keepdims=True)
    sums = jnp.where(
        lane_at == 0,
        picked[0],
        jnp.where(lane_at == 1, picked[1], jnp.where(lane_at == 2, squares, 0.0)),
    ).T
    sums_out[...] = sums[0:8, :]
    sums_in[x] = sums[0:8, :]

    def sums_copy(b):
        return pltpu.make_async_remote_copy(
            src_ref=sums_out,
            dst_ref=sums_in.at[x],
            send_sem=sums_send.at[b],
            recv_sem=sums_recv.at[x],
            device_id=peer(0, b),
            device_id_type=MESH,
        )

    def sums_arrive(b):
        source = lax.rem(x + b, nx)
        return pltpu.make_async_remote_copy(
            src_ref=sums_out,
            dst_ref=sums_in.at[source],
            send_sem=sums_send.at[b],
            recv_sem=sums_recv.at[source],
            device_id=peer(0, b),
            device_id_type=MESH,
        )

    for b in range(1, nx):
        sums_copy(b).start()
    for b in range(1, nx):
        sums_arrive(b).wait_recv()
    added = sums_in[0]
    for b in range(1, nx):
        added = added + sums_in[b]
    inverse = lax.rsqrt(added[2:3, :] / (width * nx) + 1e-06)
    probs = [jax.nn.sigmoid(added[i : i + 1, :] * inverse) for i in range(2)]
    gates = [p / (probs[0] + probs[1]) for p in probs]
    slot_inverse = jnp.sum(place_all * inverse, axis=1, keepdims=True)
    slot_inverse = jnp.broadcast_to(slot_inverse, place_all.shape)
    for e in range(nx):
        inverse_out[e] = slot_inverse[e * CAP : (e + 1) * CAP, :]
    inverse_in[s] = inverse_out[x]

    def inverse_copy(a):
        return pltpu.make_async_remote_copy(
            src_ref=inverse_out.at[x],
            dst_ref=inverse_in.at[s],
            send_sem=inverse_send.at[a],
            recv_sem=inverse_recv.at[s],
            device_id=peer(a, 0),
            device_id_type=MESH,
        )

    def inverse_arrive(a):
        source = lax.rem(s + a, ns)
        return pltpu.make_async_remote_copy(
            src_ref=inverse_out.at[x],
            dst_ref=inverse_in.at[source],
            send_sem=inverse_send.at[a],
            recv_sem=inverse_recv.at[source],
            device_id=peer(a, 0),
            device_id_type=MESH,
        )

    for a in range(1, ns):
        inverse_copy(a).start()

    weighted = jnp.concatenate(
        [
            place[e]
            * (
                jnp.where(id_rows[0] == e, gates[0], 0.0)
                + jnp.where(id_rows[1] == e, gates[1], 0.0)
            )
            for e in range(nx)
        ],
        axis=0,
    )
    slots = nx * CAP
    padded[...] = jnp.zeros_like(padded)
    padded[:slots, :] = weighted
    weighted = padded[...].T[:, :slots]
    weighted_high = weighted.astype(BF16)
    weighted_low = (weighted - weighted_high.astype(F32)).astype(BF16)

    for copy in weight_copies:
        copy.wait()
    for b in range(nx):
        source = lax.rem(x + b, nx)
        for a in range(ns):
            if (a, b) != (0, 0):
                slots_arrive(lax.rem(s + a, ns), source).wait_recv()
        arrived = [slots_in[i, source].astype(F32) for i in range(ns)]
        for h in range(2):
            chunk = jnp.concatenate([p[h * CAP : (h + 1) * CAP] for p in arrived], axis=0)
            start = pl.multiple_of(source * width + h * half, half)
            product = jnp.dot(
                chunk.astype(BF16), weights_in[pl.ds(start, half), :], preferred_element_type=F32
            )
            if b == 0 and h == 0:
                total_in[...] = product
            else:
                total_in[...] += product
    for a in range(1, ns):
        inverse_arrive(a).wait_recv()
    scale = jnp.concatenate([inverse_in[i] for i in range(ns)], axis=0)[:, :1]
    gate = total_in[:, :ff] * scale
    up = total_in[:, ff:] * scale
    hidden_all[s] = (jax.nn.silu(gate) * up).astype(BF16)

    def hidden_copy(a):
        return pltpu.make_async_remote_copy(
            src_ref=hidden_all.at[s],
            dst_ref=hidden_all.at[s],
            send_sem=hidden_send.at[a],
            recv_sem=hidden_recv.at[s],
            device_id=peer(a, 0),
            device_id_type=MESH,
        )

    def hidden_arrive(a):
        source = lax.rem(s + a, ns)
        return pltpu.make_async_remote_copy(
            src_ref=hidden_all.at[s],
            dst_ref=hidden_all.at[source],
            send_sem=hidden_send.at[a],
            recv_sem=hidden_recv.at[source],
            device_id=peer(a, 0),
            device_id_type=MESH,
        )

    for a in range(1, ns):
        hidden_copy(a).start()
    for copy in down_copies:
        copy.wait()
    for a in range(ns):
        source = lax.rem(s + a, ns)
        if a:
            hidden_arrive(a).wait_recv()
        start = pl.multiple_of(source * ff, HEAD)
        product = jnp.dot(
            hidden_all[source], weights_down[pl.ds(start, ff), :], preferred_element_type=F32
        )
        if a == 0:
            total_out[...] = product
        else:
            total_out[...] += product

    for b in range(ns):
        at = slice(b * CAP, (b + 1) * CAP)
        back_out[b] = jnp.concatenate(
            [total_out[at, :half], total_out[at, half:]], axis=0
        ).astype(BF16)

    def back_copy(block):
        return pltpu.make_async_remote_copy(
            src_ref=back_out.at[block],
            dst_ref=back_in.at[x],
            send_sem=back_send.at[block],
            recv_sem=back_recv.at[x],
            device_id={"seq": block, "exp": s},
            device_id_type=MESH,
        )

    def back_arrive(e):
        return pltpu.make_async_remote_copy(
            src_ref=back_out.at[0],
            dst_ref=back_in.at[e],
            send_sem=back_send.at[0],
            recv_sem=back_recv.at[e],
            device_id={"seq": x, "exp": e},
            device_id_type=MESH,
        )

    for a in range(ns):
        block = lax.rem(s + a, ns)
        if a:
            back_copy(block).start()
        else:

            @pl.when(x != s)
            def _():
                back_copy(block).start()

            @pl.when(x == s)
            def _():
                back_in[x] = back_out[block]

    for b in range(nx):
        e = lax.rem(x + b, nx)
        if b:
            back_arrive(e).wait_recv()
        else:

            @pl.when(x != s)
            def _():
                back_arrive(e).wait_recv()

    returned = [back_in[e].astype(F32) for e in range(nx)]
    for h in range(2):
        expert_out = jnp.concatenate(
            [r[h * CAP : (h + 1) * CAP] for r in returned], axis=0
        ).astype(BF16)
        combined = jnp.dot(weighted_high, expert_out, preferred_element_type=F32) + jnp.dot(
            weighted_low, expert_out, preferred_element_type=F32
        )
        at = slice(h * half, (h + 1) * half)
        out[:, at] = (mixed[:, at].astype(F32) + combined).astype(BF16)

    @pl.when(s < ns - 1)
    def _():
        for i in range(heads // group):
            chain_copy(i).wait_send()

    for a, b in peers:
        slots_copy(a, b).wait_send()
    for b in range(1, nx):
        sums_copy(b).wait_send()
    for a in range(1, ns):
        inverse_copy(a).wait_send()
        hidden_copy(a).wait_send()
    for a in range(ns):
        block = lax.rem(s + a, ns)
        if a:
            back_copy(block).wait_send()
        else:

            @pl.when(x != s)
            def _():
                back_copy(block).wait_send()


def fused_body(
    residual,
    query_rows,
    key_rows,
    value_rows,
    log_decay,
    attn_gain,
    norm_gain,
    router,
    expert_ids,
    priority,
    gate_weight,
    up_weight,
    down_weight,
):
    ns, nx = lax.axis_size("seq"), lax.axis_size("exp")
    rows, width = residual.shape
    heads = width // HEAD
    group = 2 if heads % 2 == 0 else 1
    steps = heads // group
    depth, ff = gate_weight.shape[1:]
    half = width // 2
    dma = pltpu.SemaphoreType.DMA
    in_vmem = pl.BlockSpec(memory_space=pltpu.VMEM)
    in_place = pl.BlockSpec(memory_space=pl.ANY)
    return pl.pallas_call(
        functools.partial(layer_kernel, ns, nx, group),
        out_shape=jax.ShapeDtypeStruct((rows, width), BF16),
        in_specs=[in_vmem] * 10 + [in_place] * 3,
        out_specs=in_vmem,
        scratch_shapes=[
            pltpu.VMEM((depth, 2 * ff), BF16),
            pltpu.VMEM(down_weight.shape[1:], BF16),
            pltpu.VMEM((rows, rows), F32),
            pltpu.VMEM((rows, rows), F32),
            pltpu.VMEM((rows, width), BF16),
            pltpu.VMEM((steps, group, HEAD, HEAD), BF16),
            pltpu.VMEM((steps, group, HEAD, HEAD), BF16),
            pltpu.VMEM((8, rows), F32),
            pltpu.VMEM((nx, 8, rows), F32),
            pltpu.VMEM((nx, 2 * CAP, half), BF16),
            pltpu.VMEM((ns, nx, 2 * CAP, half), BF16),
            pltpu.VMEM((nx, CAP, rows), F32),
            pltpu.VMEM((ns, CAP, rows), F32),
            pltpu.VMEM((ns * CAP, 2 * ff), F32),
            pltpu.VMEM((ns, ns * CAP, ff), BF16),
            pltpu.VMEM((ns * CAP, width), F32),
            pltpu.VMEM((ns, 2 * CAP, half), BF16),
            pltpu.VMEM((nx, 2 * CAP, half), BF16),
            dma((3, WEIGHT_CUTS)),
            dma((2, steps)),
            dma((nx,)),
            dma((nx,)),
            dma((ns, nx)),
            dma((ns, nx)),
            dma((ns,)),
            dma((ns,)),
            dma((ns,)),
            dma((ns,)),
            dma((ns,)),
            dma((nx,)),
        ],
        compiler_params=pltpu.CompilerParams(
            collective_id=0, has_side_effects=True, vmem_limit_bytes=60 * 1024 * 1024
        ),
        cost_estimate=pl.CostEstimate(
            flops=6 * ns * CAP * depth * ff,
            bytes_accessed=6 * depth * ff,
            transcendentals=heads * rows * rows,
        ),
    )(
        residual,
        query_rows,
        key_rows,
        value_rows,
        log_decay,
        attn_gain.reshape(1, width),
        norm_gain.reshape(1, width),
        router,
        expert_ids,
        priority,
        gate_weight,
        up_weight,
        down_weight,
    )


def body(*args):
    rows, width = args[0].shape
    ff, columns = args[10].shape[2], args[12].shape[2]
    aligned = (
        rows == HEAD
        and ff % HEAD == 0
        and width % (2 * HEAD) == 0
        and columns == width
        and args[10].shape[0] == 1
        and lax.axis_size("seq") == lax.axis_size("exp")
    )
    return (fused_body if aligned else plain_body)(*args)


def solution(mesh):
    return jax.shard_map(
        body,
        mesh=mesh,
        in_specs=(
            P(("groups", "seq"), "exp"),
            P(("groups", "seq"), "exp"),
            P(("groups", "seq"), "exp"),
            P(("groups", "seq"), "exp"),
            P(("groups", "seq"), "exp"),
            P("exp"),
            P("exp"),
            P("exp", None),
            P(("groups", "seq"), None),
            P(("groups", "seq"), None),
            P("exp", None, "seq"),
            P("exp", None, "seq"),
            P("exp", None, "seq"),
        ),
        out_specs=P(("groups", "seq"), "exp"),
        check_vma=False,
    )
```

```python
import functools

import jax
import jax.numpy as jnp
from jax import lax
from jax.experimental import pallas as pl
from jax.experimental.pallas import tpu as pltpu
from jax.sharding import PartitionSpec as P

D = 6144
HEAD = 128
EXPERTS = 32
CAP = 8


def link_states(earlier, later):
    return (earlier[0] * later[0], later[0] * earlier[1] + later[1])


def plain_body(
    residual,
    query_rows,
    key_rows,
    value_rows,
    log_decay,
    attn_gain,
    norm_gain,
    router,
    expert_ids,
    priority,
    gate_weight,
    up_weight,
    down_weight,
):
    rows = residual.shape[0]
    width = residual.shape[1]
    heads = width // HEAD
    held = lax.axis_size("exp")
    queries = query_rows.reshape(rows, heads, HEAD)
    keys_local = key_rows.reshape(rows, heads, HEAD)
    values = value_rows.reshape(rows, heads, HEAD)
    cumulative = jnp.cumsum(log_decay, axis=0)
    scores = jnp.einsum("thd,shd->hts", queries, keys_local, preferred_element_type=jnp.float32)
    causal = (jnp.arange(rows)[:, None] >= jnp.arange(rows)[None, :])[None]
    spread = cumulative.T[:, :, None] - cumulative.T[:, None, :]
    weights = jnp.where(causal, scores * jnp.exp(jnp.where(causal, spread, 0.0)), 0.0).astype(
        jnp.bfloat16
    )
    local_part = jnp.einsum("hts,shd->thd", weights, values, preferred_element_type=jnp.float32)
    to_end = jnp.exp(cumulative[-1][None, :] - cumulative)
    keyed = (keys_local.astype(jnp.float32) * to_end[:, :, None]).astype(jnp.bfloat16)
    block_state = jnp.einsum("thd,the->hde", keyed, values, preferred_element_type=jnp.float32)
    block_decay = jnp.exp(cumulative[-1])
    seq_count = lax.axis_size("seq")
    share_size = block_state.size // seq_count
    flat_state = block_state.reshape(seq_count, share_size)
    tiled_decay = jnp.broadcast_to(block_decay[None, :], (seq_count, heads))
    arrived_state, arrived_decay = (
        lax.all_to_all(flat_state, "seq", split_axis=0, concat_axis=0, tiled=True),
        lax.all_to_all(tiled_decay, "seq", split_axis=0, concat_axis=0, tiled=True),
    )
    position = lax.axis_index("seq") * share_size + jnp.arange(share_size, dtype=jnp.int32)
    owner_head = position // (HEAD * HEAD)
    selector = jnp.where(
        owner_head[None, :] == jnp.arange(heads, dtype=jnp.int32)[:, None], 1.0, 0.0
    ).astype(jnp.float32)
    element_decay = jnp.dot(arrived_decay, selector, precision=lax.Precision.HIGHEST)
    inclusive = lax.associative_scan(link_states, (element_decay, arrived_state), axis=0)[1]
    exclusive = jnp.concatenate([jnp.zeros((1, share_size), jnp.float32), inclusive[:-1]], axis=0)
    returned_prefix = lax.all_to_all(exclusive, "seq", split_axis=0, concat_axis=0, tiled=True)
    prior_state = returned_prefix.reshape(block_state.shape)
    inter = jnp.einsum(
        "thd,hde->the", queries.astype(jnp.float32), prior_state, precision=lax.Precision.HIGHEST
    )
    attended = local_part + jnp.exp(cumulative)[:, :, None] * inter
    normed = attended * lax.rsqrt(jnp.mean(attended * attended, axis=-1, keepdims=True) + 1e-06)
    normed = normed * attn_gain.reshape(heads, HEAD)
    mixed = (residual.astype(jnp.float32) + normed.reshape(rows, width)).astype(jnp.bfloat16)
    mixed_f = mixed.astype(jnp.float32)
    gained = mixed_f * norm_gain
    router_f = router.astype(jnp.float32)
    squares = lax.psum(jnp.sum(mixed_f * mixed_f, axis=1), "exp")
    inverse = lax.rsqrt(squares / D + 1e-06)
    scaled = gained * inverse[:, None]
    logits = lax.psum(jnp.dot(scaled, router_f, precision=lax.Precision.HIGHEST), "exp")
    tokens_in = scaled.astype(jnp.bfloat16)
    probs = jax.nn.sigmoid(logits)
    chosen = expert_ids[:, :, None] == jnp.arange(EXPERTS, dtype=jnp.int32)[None, None, :]
    selected = jnp.sum(jnp.where(chosen, probs[:, None, :], 0.0), axis=-1)
    gates = selected / jnp.sum(selected, axis=-1, keepdims=True)
    is_held = expert_ids[:, :, None] == jnp.arange(held, dtype=jnp.int32)[None, None, :]
    member = jnp.where(jnp.any(is_held, axis=1), 1.0, 0.0).astype(jnp.float32)
    gate_held = jnp.sum(jnp.where(is_held, gates[:, :, None], 0.0), axis=1)
    order = priority[0]
    earlier = jnp.where(order[None, :] < order[:, None], 1.0, 0.0).astype(jnp.bfloat16)
    rank = jnp.dot(earlier, member.astype(jnp.bfloat16), preferred_element_type=jnp.float32)
    kept = (member > 0.5) & (rank < CAP)
    slot_ids = jnp.arange(CAP).astype(jnp.float32)
    place = kept.T[:, None, :] & (rank.T[:, None, :] == slot_ids[None, :, None])
    place_f = jnp.where(place, 1.0, 0.0).astype(jnp.float32)
    buffer = jnp.einsum(
        "ect,td->ecd", place_f.astype(jnp.bfloat16), tokens_in, preferred_element_type=jnp.float32
    ).astype(jnp.bfloat16)
    arrived = lax.all_to_all(buffer, "exp", split_axis=0, concat_axis=2, tiled=True)[0]
    gathered = lax.all_gather(arrived, "seq", axis=0, tiled=True)
    gate = jnp.dot(gathered, gate_weight[0], preferred_element_type=jnp.float32)
    up = jnp.dot(gathered, up_weight[0], preferred_element_type=jnp.float32)
    hidden = (jax.nn.silu(gate) * up).astype(jnp.bfloat16)
    weight_rows = down_weight[0]
    summed = jnp.dot(
        lax.all_gather(hidden, "seq", axis=1, tiled=True),
        weight_rows,
        preferred_element_type=jnp.float32,
    )
    expert_out = summed.astype(jnp.bfloat16)
    returned = lax.all_to_all(expert_out, "seq", split_axis=0, concat_axis=1, tiled=True)
    regrouped = lax.all_to_all(returned[None], "exp", split_axis=2, concat_axis=0, tiled=True)
    weighted = place_f * gate_held.T[:, None, :]
    combined = jnp.einsum(
        "ect,ecd->td", weighted, regrouped.astype(jnp.float32), precision=lax.Precision.HIGHEST
    )
    return (mixed_f + combined).astype(jnp.bfloat16)


MESH = pl.DeviceIdType.MESH
F32 = jnp.float32
BF16 = jnp.bfloat16
WEIGHT_CUTS = 4


def layer_kernel(
    ns,
    nx,
    group,
    parts,
    residual,
    query,
    key,
    value,
    log_decay,
    attn_gain,
    norm_gain,
    router,
    ids,
    priority,
    gate_hbm,
    up_hbm,
    down_hbm,
    out,
    weights_in,
    weights_down,
    padded,
    cum_rows,
    mixed,
    chain_out,
    chain_in,
    sums_out,
    sums_in,
    slots_out,
    slots_in,
    inverse_out,
    inverse_in,
    total_in,
    hidden_all,
    total_out,
    back_out,
    back_in,
    chunks,
    weight_sems,
    chain_sems,
    sums_send,
    sums_recv,
    slots_send,
    slots_recv,
    inverse_send,
    inverse_recv,
    hidden_send,
    hidden_recv,
    back_send,
    back_recv,
):
    rows, width = residual.shape
    heads = width // HEAD
    half = width // 2
    depth = weights_in.shape[0]
    ff = gate_hbm.shape[2]
    span = ff // parts
    s = lax.axis_index("seq")
    x = lax.axis_index("exp")

    weight_copies = []
    cut = depth // WEIGHT_CUTS
    for i in range(WEIGHT_CUTS):
        at = pl.ds(i * cut, cut)
        for p in range(parts):
            for j, source in enumerate((gate_hbm, up_hbm)):
                weight_copies.append(
                    pltpu.make_async_copy(
                        source.at[0, at, pl.ds(p * span, span)],
                        weights_in.at[at, pl.ds((2 * p + j) * span, span)],
                        weight_sems.at[j * parts + p, i],
                    )
                )
    down_copies = []
    cut = weights_down.shape[0] // WEIGHT_CUTS
    for i in range(WEIGHT_CUTS):
        at = pl.ds(i * cut, cut)
        down_copies.append(
            pltpu.make_async_copy(down_hbm.at[0, at, :], weights_down.at[at, :], weight_sems.at[2 * parts, i])
        )
    for copy in weight_copies + down_copies:
        copy.start()

    barrier = pltpu.get_barrier_semaphore()
    peers = [(a, b) for a in range(ns) for b in range(nx) if (a, b) != (0, 0)]

    def peer(a, b):
        return {"seq": lax.rem(s + a, ns), "exp": lax.rem(x + b, nx)}

    for a, b in peers:
        pl.semaphore_signal(barrier, inc=1, device_id=peer(a, b), device_id_type=MESH)

    row_at = lax.broadcasted_iota(jnp.int32, (rows, rows), 0)
    lane_at = lax.broadcasted_iota(jnp.int32, (rows, rows), 1)
    id_rows = [ids[i : i + 1, :].astype(F32) for i in range(2)]
    order = jnp.broadcast_to(priority[...].astype(F32), (rows, rows))
    earlier = jnp.where(order.T < order, 1.0, 0.0).astype(BF16)
    expert_rows = -(-nx // 8) * 8
    expert_at = lax.broadcasted_iota(jnp.int32, (expert_rows, rows), 0).astype(F32)
    member = jnp.where((id_rows[0] == expert_at) | (id_rows[1] == expert_at), 1.0, 0.0)
    rank = jnp.dot(member.astype(BF16), earlier, preferred_element_type=F32)
    slot_at = lax.broadcasted_iota(jnp.int32, (CAP, rows), 0).astype(F32)
    rank = jnp.where(member > 0.5, rank, -1.0)
    place = [jnp.where(rank[e : e + 1, :] == slot_at, 1.0, 0.0) for e in range(nx)]
    place_all = jnp.concatenate(place, axis=0)

    padded[...] = jnp.zeros_like(padded)
    padded[:heads, :] = log_decay[...]
    upper = jnp.where(row_at <= lane_at, 1.0, 0.0).astype(F32)
    cumulative = jnp.dot(
        padded[...], upper, precision=lax.Precision.HIGHEST, preferred_element_type=F32
    )
    cum_rows[...] = cumulative
    padded[...] = cumulative.T

    @pl.when(s == 0)
    def _():
        chain_in[...] = jnp.zeros_like(chain_in)

    pl.semaphore_wait(barrier, len(peers))

    def chain_copy(i):
        return pltpu.make_async_remote_copy(
            src_ref=chain_out.at[i],
            dst_ref=chain_in.at[i],
            send_sem=chain_sems.at[0, i],
            recv_sem=chain_sems.at[1, i],
            device_id={"seq": lax.rem(s + 1, ns)},
            device_id_type=MESH,
        )

    causal = row_at >= lane_at

    def attend(i, carry):
        held = []
        for g in range(group):
            head = i * group + g
            at = pl.ds(pl.multiple_of(head * HEAD, HEAD), HEAD)
            col = jnp.sum(jnp.where(lane_at == head, padded[...], 0.0), axis=1, keepdims=True)
            row = cum_rows[pl.ds(head, 1), :]
            last = col[rows - 1 : rows, :]
            q, k, v = query[:, at], key[:, at], value[:, at]
            keyed = (k.astype(F32) * jnp.exp(last - col)).astype(BF16)
            state = lax.dot_general(
                keyed, v, (((0,), (0,)), ((), ())), preferred_element_type=F32
            )
            scores = lax.dot_general(q, k, (((1,), (1,)), ((), ())), preferred_element_type=F32)
            spread = jnp.where(causal, col - row, 0.0)
            weights = jnp.where(causal, scores * jnp.exp(spread), 0.0).astype(BF16)
            local = jnp.dot(weights, v, preferred_element_type=F32)
            held.append((at, q, state, jnp.exp(last), local, jnp.exp(col), head))

        @pl.when(s > 0)
        def _():
            chain_copy(i).wait_recv()

        @pl.when(s < ns - 1)
        def _():
            for g in range(group):
                prior = chain_in[i, g].astype(F32)
                chain_out[i, g] = (held[g][3] * prior + held[g][2]).astype(BF16)
            chain_copy(i).start()

        for g in range(group):
            at, q, _, _, local, grown, head = held[g]
            inter = jnp.dot(q, chain_in[i, g], preferred_element_type=F32)
            attended = local + grown * inter
            mean = jnp.sum(attended * attended, axis=1, keepdims=True) / HEAD
            normed = attended * lax.rsqrt(mean + 1e-06) * attn_gain[pl.ds(head, 1), :]
            mixed[:, at] = (residual[:, at].astype(F32) + normed).astype(BF16)
        return carry

    def slots_copy(m, a, b):
        return pltpu.make_async_remote_copy(
            src_ref=slots_out.at[m, lax.rem(x + b, nx)],
            dst_ref=slots_in.at[m, s, x],
            send_sem=slots_send.at[m, a, b],
            recv_sem=slots_recv.at[m, s, x],
            device_id=peer(a, b),
            device_id_type=MESH,
        )

    def slots_arrive(m, block, source):
        return pltpu.make_async_remote_copy(
            src_ref=slots_out.at[m, 0],
            dst_ref=slots_in.at[m, block, source],
            send_sem=slots_send.at[m, 0, 0],
            recv_sem=slots_recv.at[m, block, source],
            device_id=peer(1, 1),
            device_id_type=MESH,
        )

    place_b = place_all.astype(BF16)
    steps = heads // group // 2
    heads_half = heads // 2
    quarter = half // 2
    logits = jnp.zeros((rows, router.shape[0]), F32)
    squares = jnp.zeros((rows, 1), F32)
    for m in range(2):
        lax.fori_loop(m * steps, (m + 1) * steps, attend, 0)
        gained = []
        for head in range(m * heads_half, (m + 1) * heads_half):
            mixed_f = mixed[:, head * HEAD : (head + 1) * HEAD].astype(F32)
            squares = squares + jnp.sum(mixed_f * mixed_f, axis=1, keepdims=True)
            gained.append(mixed_f * norm_gain[head : head + 1, :])
        gained = jnp.concatenate(gained, axis=1)
        tokens = gained.astype(BF16)
        picked = jnp.dot(place_b, tokens, preferred_element_type=F32)
        for e in range(nx):
            at = slice(e * CAP, (e + 1) * CAP)
            slots_out[m, e] = jnp.concatenate(
                [picked[at, :quarter], picked[at, quarter:]], axis=0
            ).astype(BF16)
        slots_in[m, s, x] = slots_out[m, x]
        for a, b in peers:
            slots_copy(m, a, b).start()
        rest = (gained - tokens.astype(F32)).astype(BF16)
        router_half = router[:, m * half : (m + 1) * half]
        for part in (tokens, rest):
            logits = logits + lax.dot_general(
                part, router_half, (((1,), (1,)), ((), ())), preferred_element_type=F32
            )

    padded[...] = jnp.zeros_like(padded)
    padded[:, : router.shape[0]] = logits
    logits_t = padded[...].T
    expert_row = row_at.astype(F32)
    chosen = [
        jnp.sum(jnp.where(expert_row == r, logits_t, 0.0), axis=0, keepdims=True) for r in id_rows
    ]
    squares_t = jnp.broadcast_to(squares, (rows, rows)).T[0:1, :]
    sums = jnp.concatenate([chosen[0], chosen[1], squares_t] + [squares_t] * 5, axis=0)
    sums_out[...] = sums
    sums_in[x] = sums

    def sums_copy(b):
        return pltpu.make_async_remote_copy(
            src_ref=sums_out,
            dst_ref=sums_in.at[x],
            send_sem=sums_send.at[b],
            recv_sem=sums_recv.at[x],
            device_id=peer(0, b),
            device_id_type=MESH,
        )

    def sums_arrive(b):
        source = lax.rem(x + b, nx)
        return pltpu.make_async_remote_copy(
            src_ref=sums_out,
            dst_ref=sums_in.at[source],
            send_sem=sums_send.at[b],
            recv_sem=sums_recv.at[source],
            device_id=peer(0, b),
            device_id_type=MESH,
        )

    for b in range(1, nx):
        sums_copy(b).start()

    def chunk_of(m, b):
        source = lax.rem(x + b, nx)
        for a in range(ns):
            if (a, b) != (0, 0):
                slots_arrive(m, lax.rem(s + a, ns), source).wait_recv()
        arrived = [slots_in[m, i, source].astype(F32) for i in range(ns)]
        return jnp.concatenate(
            [
                jnp.concatenate([r[h * CAP : (h + 1) * CAP] for r in arrived], axis=0)
                for h in range(2)
            ],
            axis=1,
        ).astype(BF16)

    def chunk_rows(m, b):
        return pl.ds(pl.multiple_of(lax.rem(x + b, nx) * width + m * half, half), half)

    for copy in weight_copies:
        copy.wait()
    for b in range(nx):
        product = jnp.dot(
            chunk_of(0, b), weights_in[chunk_rows(0, b), :], preferred_element_type=F32
        )
        if b == 0:
            total_in[...] = product
        else:
            total_in[...] += product

    for b in range(1, nx):
        sums_arrive(b).wait_recv()
    added = sums_in[0]
    for b in range(1, nx):
        added = added + sums_in[b]
    inverse = lax.rsqrt(added[2:3, :] / (width * nx) + 1e-06)
    slot_inverse = jnp.sum(place_all * inverse, axis=1, keepdims=True)
    slot_inverse = jnp.broadcast_to(slot_inverse, place_all.shape)
    for e in range(nx):
        inverse_out[e] = slot_inverse[e * CAP : (e + 1) * CAP, :]
    inverse_in[s] = inverse_out[x]

    def inverse_copy(a):
        return pltpu.make_async_remote_copy(
            src_ref=inverse_out.at[x],
            dst_ref=inverse_in.at[s],
            send_sem=inverse_send.at[a],
            recv_sem=inverse_recv.at[s],
            device_id=peer(a, 0),
            device_id_type=MESH,
        )

    def inverse_arrive(a):
        source = lax.rem(s + a, ns)
        return pltpu.make_async_remote_copy(
            src_ref=inverse_out.at[x],
            dst_ref=inverse_in.at[source],
            send_sem=inverse_send.at[a],
            recv_sem=inverse_recv.at[source],
            device_id=peer(a, 0),
            device_id_type=MESH,
        )

    for a in range(1, ns):
        inverse_copy(a).start()

    for b in range(nx):
        chunks[b] = chunk_of(1, b)
    for a in range(1, ns):
        inverse_arrive(a).wait_recv()
    scale = jnp.concatenate([inverse_in[i] for i in range(ns)], axis=0)[:, :1]

    def hidden_copy(p, a):
        return pltpu.make_async_remote_copy(
            src_ref=hidden_all.at[s, p],
            dst_ref=hidden_all.at[s, p],
            send_sem=hidden_send.at[p, a],
            recv_sem=hidden_recv.at[p, s],
            device_id=peer(a, 0),
            device_id_type=MESH,
        )

    def hidden_arrive(p, a):
        source = lax.rem(s + a, ns)
        return pltpu.make_async_remote_copy(
            src_ref=hidden_all.at[s, p],
            dst_ref=hidden_all.at[source, p],
            send_sem=hidden_send.at[p, a],
            recv_sem=hidden_recv.at[p, source],
            device_id=peer(a, 0),
            device_id_type=MESH,
        )

    for p in range(parts):
        at = slice(2 * p * span, 2 * (p + 1) * span)
        product = total_in[:, at]
        for b in range(nx):
            product = product + jnp.dot(
                chunks[b], weights_in[chunk_rows(1, b), at], preferred_element_type=F32
            )
        product = product * scale
        hidden_all[s, p] = (jax.nn.silu(product[:, :span]) * product[:, span:]).astype(BF16)
        for a in range(1, ns):
            hidden_copy(p, a).start()

    probs = [jax.nn.sigmoid(added[i : i + 1, :] * inverse) for i in range(2)]
    gates = [r / (probs[0] + probs[1]) for r in probs]
    weighted = jnp.concatenate(
        [
            place[e]
            * (
                jnp.where(id_rows[0] == e, gates[0], 0.0)
                + jnp.where(id_rows[1] == e, gates[1], 0.0)
            )
            for e in range(nx)
        ],
        axis=0,
    )
    slots = nx * CAP
    padded[...] = jnp.zeros_like(padded)
    padded[:slots, :] = weighted
    weighted = padded[...].T[:, :slots]
    weighted_high = weighted.astype(BF16)
    weighted_low = (weighted - weighted_high.astype(F32)).astype(BF16)

    for copy in down_copies:
        copy.wait()
    for a in range(ns):
        source = lax.rem(s + a, ns)
        if a:
            for p in range(parts):
                hidden_arrive(p, a).wait_recv()
        start = pl.multiple_of(source * ff, HEAD)
        hidden = jnp.concatenate([hidden_all[source, p] for p in range(parts)], axis=1)
        product = jnp.dot(hidden, weights_down[pl.ds(start, ff), :], preferred_element_type=F32)
        if a == 0:
            total_out[...] = product
        else:
            total_out[...] += product

    for b in range(ns):
        at = slice(b * CAP, (b + 1) * CAP)
        back_out[b] = jnp.concatenate(
            [total_out[at, :half], total_out[at, half:]], axis=0
        ).astype(BF16)

    def back_copy(block):
        return pltpu.make_async_remote_copy(
            src_ref=back_out.at[block],
            dst_ref=back_in.at[x],
            send_sem=back_send.at[block],
            recv_sem=back_recv.at[x],
            device_id={"seq": block, "exp": s},
            device_id_type=MESH,
        )

    def back_arrive(e):
        return pltpu.make_async_remote_copy(
            src_ref=back_out.at[0],
            dst_ref=back_in.at[e],
            send_sem=back_send.at[0],
            recv_sem=back_recv.at[e],
            device_id={"seq": x, "exp": e},
            device_id_type=MESH,
        )

    for a in range(ns):
        block = lax.rem(s + a, ns)
        if a:
            back_copy(block).start()
        else:

            @pl.when(x != s)
            def _():
                back_copy(block).start()

            @pl.when(x == s)
            def _():
                back_in[x] = back_out[block]

    for b in range(nx):
        e = lax.rem(x + b, nx)
        if b:
            back_arrive(e).wait_recv()
        else:

            @pl.when(x != s)
            def _():
                back_arrive(e).wait_recv()

    returned = [back_in[e].astype(F32) for e in range(nx)]
    for h in range(2):
        expert_out = jnp.concatenate(
            [r[h * CAP : (h + 1) * CAP] for r in returned], axis=0
        ).astype(BF16)
        combined = jnp.dot(weighted_high, expert_out, preferred_element_type=F32) + jnp.dot(
            weighted_low, expert_out, preferred_element_type=F32
        )
        at = slice(h * half, (h + 1) * half)
        out[:, at] = (mixed[:, at].astype(F32) + combined).astype(BF16)

    @pl.when(s < ns - 1)
    def _():
        for i in range(heads // group):
            chain_copy(i).wait_send()

    for m in range(2):
        for a, b in peers:
            slots_copy(m, a, b).wait_send()
    for b in range(1, nx):
        sums_copy(b).wait_send()
    for a in range(1, ns):
        inverse_copy(a).wait_send()
        for p in range(parts):
            hidden_copy(p, a).wait_send()
    for a in range(ns):
        block = lax.rem(s + a, ns)
        if a:
            back_copy(block).wait_send()
        else:

            @pl.when(x != s)
            def _():
                back_copy(block).wait_send()


def fused_body(
    residual,
    query_rows,
    key_rows,
    value_rows,
    log_decay,
    attn_gain,
    norm_gain,
    router,
    expert_ids,
    priority,
    gate_weight,
    up_weight,
    down_weight,
):
    ns, nx = lax.axis_size("seq"), lax.axis_size("exp")
    rows, width = residual.shape
    heads = width // HEAD
    group = 2 if heads % 4 == 0 else 1
    steps = heads // group
    depth, ff = gate_weight.shape[1:]
    half = width // 2
    parts = next(n for n in (3, 2, 1) if ff % (n * HEAD) == 0)
    dma = pltpu.SemaphoreType.DMA
    in_vmem = pl.BlockSpec(memory_space=pltpu.VMEM)
    in_place = pl.BlockSpec(memory_space=pl.ANY)
    return pl.pallas_call(
        functools.partial(layer_kernel, ns, nx, group, parts),
        out_shape=jax.ShapeDtypeStruct((rows, width), BF16),
        in_specs=[in_vmem] * 10 + [in_place] * 3,
        out_specs=in_vmem,
        scratch_shapes=[
            pltpu.VMEM((depth, 2 * ff), BF16),
            pltpu.VMEM(down_weight.shape[1:], BF16),
            pltpu.VMEM((rows, rows), F32),
            pltpu.VMEM((rows, rows), F32),
            pltpu.VMEM((rows, width), BF16),
            pltpu.VMEM((steps, group, HEAD, HEAD), BF16),
            pltpu.VMEM((steps, group, HEAD, HEAD), BF16),
            pltpu.VMEM((8, rows), F32),
            pltpu.VMEM((nx, 8, rows), F32),
            pltpu.VMEM((2, nx, 2 * CAP, half // 2), BF16),
            pltpu.VMEM((2, ns, nx, 2 * CAP, half // 2), BF16),
            pltpu.VMEM((nx, CAP, rows), F32),
            pltpu.VMEM((ns, CAP, rows), F32),
            pltpu.VMEM((ns * CAP, 2 * ff), F32),
            pltpu.VMEM((ns, parts, ns * CAP, ff // parts), BF16),
            pltpu.VMEM((ns * CAP, width), F32),
            pltpu.VMEM((ns, 2 * CAP, half), BF16),
            pltpu.VMEM((nx, 2 * CAP, half), BF16),
            pltpu.VMEM((nx, ns * CAP, half), BF16),
            dma((2 * parts + 1, WEIGHT_CUTS)),
            dma((2, steps)),
            dma((nx,)),
            dma((nx,)),
            dma((2, ns, nx)),
            dma((2, ns, nx)),
            dma((ns,)),
            dma((ns,)),
            dma((parts, ns)),
            dma((parts, ns)),
            dma((ns,)),
            dma((nx,)),
        ],
        compiler_params=pltpu.CompilerParams(
            collective_id=0, has_side_effects=True, vmem_limit_bytes=60 * 1024 * 1024
        ),
        cost_estimate=pl.CostEstimate(
            flops=6 * ns * CAP * depth * ff,
            bytes_accessed=6 * depth * ff,
            transcendentals=heads * rows * rows,
        ),
    )(
        residual,
        query_rows,
        key_rows,
        value_rows,
        log_decay.T,
        attn_gain.reshape(heads, HEAD),
        norm_gain.reshape(heads, HEAD),
        router.T,
        expert_ids.T,
        priority,
        gate_weight,
        up_weight,
        down_weight,
    )


def body(*args):
    rows, width = args[0].shape
    ff, columns = args[10].shape[2], args[12].shape[2]
    aligned = (
        rows == HEAD
        and ff % HEAD == 0
        and width % (4 * HEAD) == 0
        and columns == width
        and args[10].shape[0] == 1
        and lax.axis_size("seq") == lax.axis_size("exp")
    )
    return (fused_body if aligned else plain_body)(*args)


def solution(mesh):
    return jax.shard_map(
        body,
        mesh=mesh,
        in_specs=(
            P(("groups", "seq"), "exp"),
            P(("groups", "seq"), "exp"),
            P(("groups", "seq"), "exp"),
            P(("groups", "seq"), "exp"),
            P(("groups", "seq"), "exp"),
            P("exp"),
            P("exp"),
            P("exp", None),
            P(("groups", "seq"), None),
            P(("groups", "seq"), None),
            P("exp", None, "seq"),
            P("exp", None, "seq"),
            P("exp", None, "seq"),
        ),
        out_specs=P(("groups", "seq"), "exp"),
        check_vma=False,
    )
```

```python
import functools

import jax
import jax.numpy as jnp
from jax import lax
from jax.experimental import pallas as pl
from jax.experimental.pallas import tpu as pltpu
from jax.sharding import PartitionSpec as P

D = 6144
HEAD = 128
EXPERTS = 32
CAP = 8


def link_states(earlier, later):
    return (earlier[0] * later[0], later[0] * earlier[1] + later[1])


def plain_body(
    residual,
    query_rows,
    key_rows,
    value_rows,
    log_decay,
    attn_gain,
    norm_gain,
    router,
    expert_ids,
    priority,
    gate_weight,
    up_weight,
    down_weight,
):
    rows = residual.shape[0]
    width = residual.shape[1]
    heads = width // HEAD
    held = lax.axis_size("exp")
    queries = query_rows.reshape(rows, heads, HEAD)
    keys_local = key_rows.reshape(rows, heads, HEAD)
    values = value_rows.reshape(rows, heads, HEAD)
    cumulative = jnp.cumsum(log_decay, axis=0)
    scores = jnp.einsum("thd,shd->hts", queries, keys_local, preferred_element_type=jnp.float32)
    causal = (jnp.arange(rows)[:, None] >= jnp.arange(rows)[None, :])[None]
    spread = cumulative.T[:, :, None] - cumulative.T[:, None, :]
    weights = jnp.where(causal, scores * jnp.exp(jnp.where(causal, spread, 0.0)), 0.0).astype(
        jnp.bfloat16
    )
    local_part = jnp.einsum("hts,shd->thd", weights, values, preferred_element_type=jnp.float32)
    to_end = jnp.exp(cumulative[-1][None, :] - cumulative)
    keyed = (keys_local.astype(jnp.float32) * to_end[:, :, None]).astype(jnp.bfloat16)
    block_state = jnp.einsum("thd,the->hde", keyed, values, preferred_element_type=jnp.float32)
    block_decay = jnp.exp(cumulative[-1])
    seq_count = lax.axis_size("seq")
    share_size = block_state.size // seq_count
    flat_state = block_state.reshape(seq_count, share_size)
    tiled_decay = jnp.broadcast_to(block_decay[None, :], (seq_count, heads))
    arrived_state, arrived_decay = (
        lax.all_to_all(flat_state, "seq", split_axis=0, concat_axis=0, tiled=True),
        lax.all_to_all(tiled_decay, "seq", split_axis=0, concat_axis=0, tiled=True),
    )
    position = lax.axis_index("seq") * share_size + jnp.arange(share_size, dtype=jnp.int32)
    owner_head = position // (HEAD * HEAD)
    selector = jnp.where(
        owner_head[None, :] == jnp.arange(heads, dtype=jnp.int32)[:, None], 1.0, 0.0
    ).astype(jnp.float32)
    element_decay = jnp.dot(arrived_decay, selector, precision=lax.Precision.HIGHEST)
    inclusive = lax.associative_scan(link_states, (element_decay, arrived_state), axis=0)[1]
    exclusive = jnp.concatenate([jnp.zeros((1, share_size), jnp.float32), inclusive[:-1]], axis=0)
    returned_prefix = lax.all_to_all(exclusive, "seq", split_axis=0, concat_axis=0, tiled=True)
    prior_state = returned_prefix.reshape(block_state.shape)
    inter = jnp.einsum(
        "thd,hde->the", queries.astype(jnp.float32), prior_state, precision=lax.Precision.HIGHEST
    )
    attended = local_part + jnp.exp(cumulative)[:, :, None] * inter
    normed = attended * lax.rsqrt(jnp.mean(attended * attended, axis=-1, keepdims=True) + 1e-06)
    normed = normed * attn_gain.reshape(heads, HEAD)
    mixed = (residual.astype(jnp.float32) + normed.reshape(rows, width)).astype(jnp.bfloat16)
    mixed_f = mixed.astype(jnp.float32)
    gained = mixed_f * norm_gain
    router_f = router.astype(jnp.float32)
    squares = lax.psum(jnp.sum(mixed_f * mixed_f, axis=1), "exp")
    inverse = lax.rsqrt(squares / D + 1e-06)
    scaled = gained * inverse[:, None]
    logits = lax.psum(jnp.dot(scaled, router_f, precision=lax.Precision.HIGHEST), "exp")
    tokens_in = scaled.astype(jnp.bfloat16)
    probs = jax.nn.sigmoid(logits)
    chosen = expert_ids[:, :, None] == jnp.arange(EXPERTS, dtype=jnp.int32)[None, None, :]
    selected = jnp.sum(jnp.where(chosen, probs[:, None, :], 0.0), axis=-1)
    gates = selected / jnp.sum(selected, axis=-1, keepdims=True)
    is_held = expert_ids[:, :, None] == jnp.arange(held, dtype=jnp.int32)[None, None, :]
    member = jnp.where(jnp.any(is_held, axis=1), 1.0, 0.0).astype(jnp.float32)
    gate_held = jnp.sum(jnp.where(is_held, gates[:, :, None], 0.0), axis=1)
    order = priority[0]
    earlier = jnp.where(order[None, :] < order[:, None], 1.0, 0.0).astype(jnp.bfloat16)
    rank = jnp.dot(earlier, member.astype(jnp.bfloat16), preferred_element_type=jnp.float32)
    kept = (member > 0.5) & (rank < CAP)
    slot_ids = jnp.arange(CAP).astype(jnp.float32)
    place = kept.T[:, None, :] & (rank.T[:, None, :] == slot_ids[None, :, None])
    place_f = jnp.where(place, 1.0, 0.0).astype(jnp.float32)
    buffer = jnp.einsum(
        "ect,td->ecd", place_f.astype(jnp.bfloat16), tokens_in, preferred_element_type=jnp.float32
    ).astype(jnp.bfloat16)
    arrived = lax.all_to_all(buffer, "exp", split_axis=0, concat_axis=2, tiled=True)[0]
    gathered = lax.all_gather(arrived, "seq", axis=0, tiled=True)
    gate = jnp.dot(gathered, gate_weight[0], preferred_element_type=jnp.float32)
    up = jnp.dot(gathered, up_weight[0], preferred_element_type=jnp.float32)
    hidden = (jax.nn.silu(gate) * up).astype(jnp.bfloat16)
    weight_rows = down_weight[0]
    summed = jnp.dot(
        lax.all_gather(hidden, "seq", axis=1, tiled=True),
        weight_rows,
        preferred_element_type=jnp.float32,
    )
    expert_out = summed.astype(jnp.bfloat16)
    returned = lax.all_to_all(expert_out, "seq", split_axis=0, concat_axis=1, tiled=True)
    regrouped = lax.all_to_all(returned[None], "exp", split_axis=2, concat_axis=0, tiled=True)
    weighted = place_f * gate_held.T[:, None, :]
    combined = jnp.einsum(
        "ect,ecd->td", weighted, regrouped.astype(jnp.float32), precision=lax.Precision.HIGHEST
    )
    return (mixed_f + combined).astype(jnp.bfloat16)


MESH = pl.DeviceIdType.MESH
F32 = jnp.float32
BF16 = jnp.bfloat16
WEIGHT_CUTS = 2


def layer_kernel(
    ns,
    nx,
    group,
    parts,
    residual,
    query,
    key,
    value,
    log_decay,
    attn_gain,
    norm_gain,
    router,
    ids,
    priority,
    gate_hbm,
    up_hbm,
    down_hbm,
    out,
    weights_in,
    weights_down,
    padded,
    cum_rows,
    mixed,
    states,
    chain_out,
    chain_in,
    sums_out,
    sums_in,
    slots_out,
    slots_in,
    inverse_out,
    inverse_in,
    total_in,
    hidden_all,
    total_out,
    back_out,
    back_in,
    chunks,
    weight_sems,
    down_sems,
    chain_sems,
    sums_send,
    sums_recv,
    slots_send,
    slots_recv,
    inverse_send,
    inverse_recv,
    hidden_send,
    hidden_recv,
    back_send,
    back_recv,
):
    rows, width = residual.shape
    heads = width // HEAD
    half = width // 2
    depth = weights_in.shape[0]
    ff = gate_hbm.shape[2]
    span = ff // parts
    s = lax.axis_index("seq")
    x = lax.axis_index("exp")

    barrier = pltpu.get_barrier_semaphore()
    peers = [(a, b) for a in range(ns) for b in range(nx) if (a, b) != (0, 0)]

    def peer(a, b):
        return {"seq": lax.rem(s + a, ns), "exp": lax.rem(x + b, nx)}

    for a, b in peers:
        pl.semaphore_signal(barrier, inc=1, device_id=peer(a, b), device_id_type=MESH)

    weight_copies = []
    cut = depth // WEIGHT_CUTS
    for i in range(WEIGHT_CUTS):
        at = pl.ds(i * cut, cut)
        for p in range(parts):
            for j, source in enumerate((gate_hbm, up_hbm)):
                weight_copies.append(
                    pltpu.make_async_copy(
                        source.at[0, at, pl.ds(p * span, span)],
                        weights_in.at[at, pl.ds((2 * p + j) * span, span)],
                        weight_sems.at[j * parts + p, i],
                    )
                )
    down_copies = []
    for p in range(parts):
        for i in range(ns):
            down_copies.append(
                pltpu.make_async_copy(
                    down_hbm.at[0, pl.ds(i * ff + p * span, span), :],
                    weights_down.at[pl.ds((p * ns + i) * span, span), :],
                    down_sems.at[p, i],
                )
            )
    for copy in weight_copies + down_copies:
        copy.start()

    row_at = lax.broadcasted_iota(jnp.int32, (rows, rows), 0)
    lane_at = lax.broadcasted_iota(jnp.int32, (rows, rows), 1)
    id_rows = [ids[i : i + 1, :].astype(F32) for i in range(2)]
    order = jnp.broadcast_to(priority[...].astype(F32), (rows, rows))
    earlier = jnp.where(order.T < order, 1.0, 0.0).astype(BF16)
    expert_rows = -(-nx // 8) * 8
    expert_at = lax.broadcasted_iota(jnp.int32, (expert_rows, rows), 0).astype(F32)
    member = jnp.where((id_rows[0] == expert_at) | (id_rows[1] == expert_at), 1.0, 0.0)
    rank = jnp.dot(member.astype(BF16), earlier, preferred_element_type=F32)
    slot_at = lax.broadcasted_iota(jnp.int32, (CAP, rows), 0).astype(F32)
    rank = jnp.where(member > 0.5, rank, -1.0)
    place = [jnp.where(rank[e : e + 1, :] == slot_at, 1.0, 0.0) for e in range(nx)]
    place_all = jnp.concatenate(place, axis=0)

    padded[...] = jnp.zeros_like(padded)
    padded[:heads, :] = log_decay[...]
    upper = jnp.where(row_at <= lane_at, 1.0, 0.0).astype(F32)
    cumulative = jnp.dot(
        padded[...], upper, precision=lax.Precision.HIGHEST, preferred_element_type=F32
    )
    cum_rows[...] = cumulative
    padded[...] = cumulative.T

    @pl.when(s == 0)
    def _():
        chain_in[...] = jnp.zeros_like(chain_in)

    pl.semaphore_wait(barrier, len(peers))

    def chain_copy(i):
        return pltpu.make_async_remote_copy(
            src_ref=chain_out.at[i],
            dst_ref=chain_in.at[i],
            send_sem=chain_sems.at[0, i],
            recv_sem=chain_sems.at[1, i],
            device_id={"seq": lax.rem(s + 1, ns)},
            device_id_type=MESH,
        )

    cluster = 2 * group
    for first in range(0, heads, cluster):
        for head in range(first, first + cluster):
            at = slice(head * HEAD, (head + 1) * HEAD)
            col = padded[:, head : head + 1]
            to_end = jnp.exp(col[rows - 1 : rows, :] - col)
            keyed = (key[:, at].astype(F32) * to_end).astype(BF16)
            state = lax.dot_general(
                keyed, value[:, at], (((0,), (0,)), ((), ())), preferred_element_type=F32
            )
            states[head] = state
            chain_out[head] = state.astype(BF16)

        @pl.when(s == 0)
        def _():
            for head in range(first, first + cluster):
                chain_copy(head).start()

    causal = row_at >= lane_at

    def attend(i, carry):
        cols = []
        for g in range(group):
            head = i * group + g
            cols.append(
                jnp.sum(jnp.where(lane_at == head, padded[...], 0.0), axis=1, keepdims=True)
            )

        @pl.when(s > 0)
        def _():
            for g in range(group):
                head = i * group + g
                chain_copy(head).wait_recv()

                @pl.when(s < ns - 1)
                def _():
                    decay = jnp.exp(cols[g][rows - 1 : rows, :])
                    prior = chain_in[head].astype(F32)
                    chain_out[head] = (decay * prior + states[head]).astype(BF16)
                    chain_copy(head).start()

        for g in range(group):
            head = i * group + g
            at = pl.ds(pl.multiple_of(head * HEAD, HEAD), HEAD)
            col, row = cols[g], cum_rows[pl.ds(head, 1), :]
            q, k, v = query[:, at], key[:, at], value[:, at]
            scores = lax.dot_general(q, k, (((1,), (1,)), ((), ())), preferred_element_type=F32)
            spread = jnp.where(causal, col - row, 0.0)
            weights = jnp.where(causal, scores * jnp.exp(spread), 0.0).astype(BF16)
            local = jnp.dot(weights, v, preferred_element_type=F32)
            inter = jnp.dot(q, chain_in[head], preferred_element_type=F32)
            attended = local + jnp.exp(col) * inter
            mean = jnp.sum(attended * attended, axis=1, keepdims=True) / HEAD
            normed = attended * lax.rsqrt(mean + 1e-06) * attn_gain[pl.ds(head, 1), :]
            mixed[:, at] = (residual[:, at].astype(F32) + normed).astype(BF16)
        return carry

    def slots_copy(m, a, b):
        return pltpu.make_async_remote_copy(
            src_ref=slots_out.at[m, lax.rem(x + b, nx)],
            dst_ref=slots_in.at[m, s, x],
            send_sem=slots_send.at[m, a, b],
            recv_sem=slots_recv.at[m, s, x],
            device_id=peer(a, b),
            device_id_type=MESH,
        )

    def slots_arrive(m, block, source):
        return pltpu.make_async_remote_copy(
            src_ref=slots_out.at[m, 0],
            dst_ref=slots_in.at[m, block, source],
            send_sem=slots_send.at[m, 0, 0],
            recv_sem=slots_recv.at[m, block, source],
            device_id=peer(1, 1),
            device_id_type=MESH,
        )

    place_b = place_all.astype(BF16)
    steps = heads // group // 2
    heads_half = heads // 2
    quarter = half // 2
    logits = jnp.zeros((rows, router.shape[0]), F32)
    squares = jnp.zeros((rows, 1), F32)
    for m in range(2):
        lax.fori_loop(m * steps, (m + 1) * steps, attend, 0)
        gained = []
        for head in range(m * heads_half, (m + 1) * heads_half):
            mixed_f = mixed[:, head * HEAD : (head + 1) * HEAD].astype(F32)
            squares = squares + jnp.sum(mixed_f * mixed_f, axis=1, keepdims=True)
            gained.append(mixed_f * norm_gain[head : head + 1, :])
        gained = jnp.concatenate(gained, axis=1)
        tokens = gained.astype(BF16)
        picked = jnp.dot(place_b, tokens, preferred_element_type=F32)
        for e in range(nx):
            at = slice(e * CAP, (e + 1) * CAP)
            slots_out[m, e] = jnp.concatenate(
                [picked[at, :quarter], picked[at, quarter:]], axis=0
            ).astype(BF16)
        slots_in[m, s, x] = slots_out[m, x]
        for a, b in peers:
            slots_copy(m, a, b).start()
        rest = (gained - tokens.astype(F32)).astype(BF16)
        router_half = router[:, m * half : (m + 1) * half]
        for part in (tokens, rest):
            logits = logits + lax.dot_general(
                part, router_half, (((1,), (1,)), ((), ())), preferred_element_type=F32
            )

    padded[...] = jnp.zeros_like(padded)
    padded[:, : router.shape[0]] = logits
    logits_t = padded[...].T
    expert_row = row_at.astype(F32)
    chosen = [
        jnp.sum(jnp.where(expert_row == r, logits_t, 0.0), axis=0, keepdims=True) for r in id_rows
    ]
    squares_t = jnp.broadcast_to(squares, (rows, rows)).T[0:1, :]
    sums = jnp.concatenate([chosen[0], chosen[1], squares_t] + [squares_t] * 5, axis=0)
    sums_out[...] = sums
    sums_in[x] = sums

    def sums_copy(b):
        return pltpu.make_async_remote_copy(
            src_ref=sums_out,
            dst_ref=sums_in.at[x],
            send_sem=sums_send.at[b],
            recv_sem=sums_recv.at[x],
            device_id=peer(0, b),
            device_id_type=MESH,
        )

    def sums_arrive(b):
        source = lax.rem(x + b, nx)
        return pltpu.make_async_remote_copy(
            src_ref=sums_out,
            dst_ref=sums_in.at[source],
            send_sem=sums_send.at[b],
            recv_sem=sums_recv.at[source],
            device_id=peer(0, b),
            device_id_type=MESH,
        )

    for b in range(1, nx):
        sums_copy(b).start()

    def slots_wait(m):
        for a, b in peers:
            slots_arrive(m, lax.rem(s + a, ns), lax.rem(x + b, nx)).wait_recv()

    def chunk_of(m, source):
        arrived = [slots_in[m, i, source].astype(F32) for i in range(ns)]
        return jnp.concatenate(
            [
                jnp.concatenate([r[h * CAP : (h + 1) * CAP] for r in arrived], axis=0)
                for h in range(2)
            ],
            axis=1,
        ).astype(BF16)

    def product_of(m, held, at):
        product = None
        for source in range(nx):
            start = source * width + m * half
            term = jnp.dot(
                held[source], weights_in[start : start + half, at], preferred_element_type=F32
            )
            product = term if product is None else product + term
        return product

    slots_wait(0)
    for copy in weight_copies:
        copy.wait()
    held = [chunk_of(0, source) for source in range(nx)]
    for p in range(parts):
        at = slice(2 * p * span, 2 * (p + 1) * span)
        total_in[:, at] = product_of(0, held, at)

    for b in range(1, nx):
        sums_arrive(b).wait_recv()
    added = sums_in[0]
    for b in range(1, nx):
        added = added + sums_in[b]
    inverse = lax.rsqrt(added[2:3, :] / (width * nx) + 1e-06)
    slot_inverse = jnp.sum(place_all * inverse, axis=1, keepdims=True)
    slot_inverse = jnp.broadcast_to(slot_inverse, place_all.shape)
    for e in range(nx):
        inverse_out[e] = slot_inverse[e * CAP : (e + 1) * CAP, :]
    inverse_in[s] = inverse_out[x]

    def inverse_copy(a):
        return pltpu.make_async_remote_copy(
            src_ref=inverse_out.at[x],
            dst_ref=inverse_in.at[s],
            send_sem=inverse_send.at[a],
            recv_sem=inverse_recv.at[s],
            device_id=peer(a, 0),
            device_id_type=MESH,
        )

    def inverse_arrive(a):
        source = lax.rem(s + a, ns)
        return pltpu.make_async_remote_copy(
            src_ref=inverse_out.at[x],
            dst_ref=inverse_in.at[source],
            send_sem=inverse_send.at[a],
            recv_sem=inverse_recv.at[source],
            device_id=peer(a, 0),
            device_id_type=MESH,
        )

    for a in range(1, ns):
        inverse_copy(a).start()

    slots_wait(1)
    for source in range(nx):
        chunks[source] = chunk_of(1, source)
    for a in range(1, ns):
        inverse_arrive(a).wait_recv()
    scale = jnp.concatenate([inverse_in[i] for i in range(ns)], axis=0)[:, :1]

    def hidden_copy(p, a):
        return pltpu.make_async_remote_copy(
            src_ref=hidden_all.at[s, p],
            dst_ref=hidden_all.at[s, p],
            send_sem=hidden_send.at[p, a],
            recv_sem=hidden_recv.at[p, s],
            device_id=peer(a, 0),
            device_id_type=MESH,
        )

    def hidden_arrive(p, a):
        source = lax.rem(s + a, ns)
        return pltpu.make_async_remote_copy(
            src_ref=hidden_all.at[s, p],
            dst_ref=hidden_all.at[source, p],
            send_sem=hidden_send.at[p, a],
            recv_sem=hidden_recv.at[p, source],
            device_id=peer(a, 0),
            device_id_type=MESH,
        )

    for p in range(parts):
        at = slice(2 * p * span, 2 * (p + 1) * span)
        product = (total_in[:, at] + product_of(1, chunks, at)) * scale
        hidden_all[s, p] = (jax.nn.silu(product[:, :span]) * product[:, span:]).astype(BF16)
        for a in range(1, ns):
            hidden_copy(p, a).start()

    probs = [jax.nn.sigmoid(added[i : i + 1, :] * inverse) for i in range(2)]
    gates = [r / (probs[0] + probs[1]) for r in probs]
    weighted = jnp.concatenate(
        [
            place[e]
            * (
                jnp.where(id_rows[0] == e, gates[0], 0.0)
                + jnp.where(id_rows[1] == e, gates[1], 0.0)
            )
            for e in range(nx)
        ],
        axis=0,
    )
    slots = nx * CAP
    padded[...] = jnp.zeros_like(padded)
    padded[:slots, :] = weighted
    weighted = padded[...].T[:, :slots]
    weighted_high = weighted.astype(BF16)
    weighted_low = (weighted - weighted_high.astype(F32)).astype(BF16)

    for copy in down_copies:
        copy.wait()

    def down_product(p, at):
        hidden = jnp.concatenate([hidden_all[i, p] for i in range(ns)], axis=1)
        return jnp.dot(
            hidden,
            weights_down[p * ns * span : (p + 1) * ns * span, at],
            preferred_element_type=F32,
        )

    def back_copy(h, block):
        return pltpu.make_async_remote_copy(
            src_ref=back_out.at[h, block],
            dst_ref=back_in.at[h, x],
            send_sem=back_send.at[h, block],
            recv_sem=back_recv.at[h, x],
            device_id={"seq": block, "exp": s},
            device_id_type=MESH,
        )

    def back_arrive(h, e):
        return pltpu.make_async_remote_copy(
            src_ref=back_out.at[h, 0],
            dst_ref=back_in.at[h, e],
            send_sem=back_send.at[h, 0],
            recv_sem=back_recv.at[h, e],
            device_id={"seq": x, "exp": e},
            device_id_type=MESH,
        )

    for p in range(parts):
        for a in range(1, ns):
            hidden_arrive(p, a).wait_recv()
        if p < parts - 1:
            product = down_product(p, slice(0, width))
            total_out[...] = product if p == 0 else total_out[...] + product
    for h in range(2):
        at = slice(h * half, (h + 1) * half)
        total = down_product(parts - 1, at)
        if parts > 1:
            total = total + total_out[:, at]
        for b in range(ns):
            of = slice(b * CAP, (b + 1) * CAP)
            back_out[h, b] = jnp.concatenate(
                [total[of, :quarter], total[of, quarter:]], axis=0
            ).astype(BF16)
        for a in range(1, ns):
            back_copy(h, lax.rem(s + a, ns)).start()

        @pl.when(x != s)
        def _():
            back_copy(h, s).start()

        @pl.when(x == s)
        def _():
            back_in[h, x] = back_out[h, s]

    for h in range(2):
        for b in range(1, nx):
            back_arrive(h, lax.rem(x + b, nx)).wait_recv()

        @pl.when(x != s)
        def _():
            back_arrive(h, x).wait_recv()

        returned = [back_in[h, e].astype(F32) for e in range(nx)]
        expert_out = jnp.concatenate(
            [
                jnp.concatenate([r[j * CAP : (j + 1) * CAP] for r in returned], axis=0)
                for j in range(2)
            ],
            axis=1,
        ).astype(BF16)
        combined = jnp.dot(weighted_high, expert_out, preferred_element_type=F32) + jnp.dot(
            weighted_low, expert_out, preferred_element_type=F32
        )
        at = slice(h * half, (h + 1) * half)
        out[:, at] = (mixed[:, at].astype(F32) + combined).astype(BF16)

    @pl.when(s < ns - 1)
    def _():
        for head in range(heads):
            chain_copy(head).wait_send()

    for m in range(2):
        for a, b in peers:
            slots_copy(m, a, b).wait_send()
    for b in range(1, nx):
        sums_copy(b).wait_send()
    for a in range(1, ns):
        inverse_copy(a).wait_send()
        for p in range(parts):
            hidden_copy(p, a).wait_send()
    for h in range(2):
        for a in range(1, ns):
            back_copy(h, lax.rem(s + a, ns)).wait_send()

        @pl.when(x != s)
        def _():
            back_copy(h, s).wait_send()


def fused_body(
    residual,
    query_rows,
    key_rows,
    value_rows,
    log_decay,
    attn_gain,
    norm_gain,
    router,
    expert_ids,
    priority,
    gate_weight,
    up_weight,
    down_weight,
):
    ns, nx = lax.axis_size("seq"), lax.axis_size("exp")
    rows, width = residual.shape
    heads = width // HEAD
    group = 2 if heads % 4 == 0 else 1
    depth, ff = gate_weight.shape[1:]
    half = width // 2
    parts = next(n for n in (3, 2, 1) if ff % (n * HEAD) == 0)
    dma = pltpu.SemaphoreType.DMA
    in_vmem = pl.BlockSpec(memory_space=pltpu.VMEM)
    in_place = pl.BlockSpec(memory_space=pl.ANY)
    return pl.pallas_call(
        functools.partial(layer_kernel, ns, nx, group, parts),
        out_shape=jax.ShapeDtypeStruct((rows, width), BF16),
        in_specs=[in_vmem] * 10 + [in_place] * 3,
        out_specs=in_vmem,
        scratch_shapes=[
            pltpu.VMEM((depth, 2 * ff), BF16),
            pltpu.VMEM(down_weight.shape[1:], BF16),
            pltpu.VMEM((rows, rows), F32),
            pltpu.VMEM((rows, rows), F32),
            pltpu.VMEM((rows, width), BF16),
            pltpu.VMEM((heads, HEAD, HEAD), F32),
            pltpu.VMEM((heads, HEAD, HEAD), BF16),
            pltpu.VMEM((heads, HEAD, HEAD), BF16),
            pltpu.VMEM((8, rows), F32),
            pltpu.VMEM((nx, 8, rows), F32),
            pltpu.VMEM((2, nx, 2 * CAP, half // 2), BF16),
            pltpu.VMEM((2, ns, nx, 2 * CAP, half // 2), BF16),
            pltpu.VMEM((nx, CAP, rows), F32),
            pltpu.VMEM((ns, CAP, rows), F32),
            pltpu.VMEM((ns * CAP, 2 * ff), F32),
            pltpu.VMEM((ns, parts, ns * CAP, ff // parts), BF16),
            pltpu.VMEM((ns * CAP, width), F32),
            pltpu.VMEM((2, ns, 2 * CAP, half // 2), BF16),
            pltpu.VMEM((2, nx, 2 * CAP, half // 2), BF16),
            pltpu.VMEM((nx, ns * CAP, half), BF16),
            dma((2 * parts, WEIGHT_CUTS)),
            dma((parts, ns)),
            dma((2, heads)),
            dma((nx,)),
            dma((nx,)),
            dma((2, ns, nx)),
            dma((2, ns, nx)),
            dma((ns,)),
            dma((ns,)),
            dma((parts, ns)),
            dma((parts, ns)),
            dma((2, ns)),
            dma((2, nx)),
        ],
        compiler_params=pltpu.CompilerParams(
            collective_id=0, has_side_effects=True, vmem_limit_bytes=60 * 1024 * 1024
        ),
        cost_estimate=pl.CostEstimate(
            flops=6 * ns * CAP * depth * ff,
            bytes_accessed=6 * depth * ff,
            transcendentals=heads * rows * rows,
        ),
    )(
        residual,
        query_rows,
        key_rows,
        value_rows,
        log_decay.T,
        attn_gain.reshape(heads, HEAD),
        norm_gain.reshape(heads, HEAD),
        router.T,
        expert_ids.T,
        priority,
        gate_weight,
        up_weight,
        down_weight,
    )


def body(*args):
    rows, width = args[0].shape
    ff, columns = args[10].shape[2], args[12].shape[2]
    aligned = (
        rows == HEAD
        and ff % HEAD == 0
        and width % (4 * HEAD) == 0
        and columns == width
        and args[10].shape[0] == 1
        and lax.axis_size("seq") == lax.axis_size("exp")
    )
    return (fused_body if aligned else plain_body)(*args)


def solution(mesh):
    return jax.shard_map(
        body,
        mesh=mesh,
        in_specs=(
            P(("groups", "seq"), "exp"),
            P(("groups", "seq"), "exp"),
            P(("groups", "seq"), "exp"),
            P(("groups", "seq"), "exp"),
            P(("groups", "seq"), "exp"),
            P("exp"),
            P("exp"),
            P("exp", None),
            P(("groups", "seq"), None),
            P(("groups", "seq"), None),
            P("exp", None, "seq"),
            P("exp", None, "seq"),
            P("exp", None, "seq"),
        ),
        out_specs=P(("groups", "seq"), "exp"),
        check_vma=False,
    )
```

```python
import functools

import jax
import jax.numpy as jnp
from jax import lax
from jax.experimental import pallas as pl
from jax.experimental.pallas import tpu as pltpu
from jax.sharding import PartitionSpec as P

D = 6144
HEAD = 128
EXPERTS = 32
CAP = 8


def link_states(earlier, later):
    return (earlier[0] * later[0], later[0] * earlier[1] + later[1])


def plain_body(
    residual,
    query_rows,
    key_rows,
    value_rows,
    log_decay,
    attn_gain,
    norm_gain,
    router,
    expert_ids,
    priority,
    gate_weight,
    up_weight,
    down_weight,
):
    rows = residual.shape[0]
    width = residual.shape[1]
    heads = width // HEAD
    held = lax.axis_size("exp")
    queries = query_rows.reshape(rows, heads, HEAD)
    keys_local = key_rows.reshape(rows, heads, HEAD)
    values = value_rows.reshape(rows, heads, HEAD)
    cumulative = jnp.cumsum(log_decay, axis=0)
    scores = jnp.einsum("thd,shd->hts", queries, keys_local, preferred_element_type=jnp.float32)
    causal = (jnp.arange(rows)[:, None] >= jnp.arange(rows)[None, :])[None]
    spread = cumulative.T[:, :, None] - cumulative.T[:, None, :]
    weights = jnp.where(causal, scores * jnp.exp(jnp.where(causal, spread, 0.0)), 0.0).astype(
        jnp.bfloat16
    )
    local_part = jnp.einsum("hts,shd->thd", weights, values, preferred_element_type=jnp.float32)
    to_end = jnp.exp(cumulative[-1][None, :] - cumulative)
    keyed = (keys_local.astype(jnp.float32) * to_end[:, :, None]).astype(jnp.bfloat16)
    block_state = jnp.einsum("thd,the->hde", keyed, values, preferred_element_type=jnp.float32)
    block_decay = jnp.exp(cumulative[-1])
    seq_count = lax.axis_size("seq")
    share_size = block_state.size // seq_count
    flat_state = block_state.reshape(seq_count, share_size)
    tiled_decay = jnp.broadcast_to(block_decay[None, :], (seq_count, heads))
    arrived_state, arrived_decay = (
        lax.all_to_all(flat_state, "seq", split_axis=0, concat_axis=0, tiled=True),
        lax.all_to_all(tiled_decay, "seq", split_axis=0, concat_axis=0, tiled=True),
    )
    position = lax.axis_index("seq") * share_size + jnp.arange(share_size, dtype=jnp.int32)
    owner_head = position // (HEAD * HEAD)
    selector = jnp.where(
        owner_head[None, :] == jnp.arange(heads, dtype=jnp.int32)[:, None], 1.0, 0.0
    ).astype(jnp.float32)
    element_decay = jnp.dot(arrived_decay, selector, precision=lax.Precision.HIGHEST)
    inclusive = lax.associative_scan(link_states, (element_decay, arrived_state), axis=0)[1]
    exclusive = jnp.concatenate([jnp.zeros((1, share_size), jnp.float32), inclusive[:-1]], axis=0)
    returned_prefix = lax.all_to_all(exclusive, "seq", split_axis=0, concat_axis=0, tiled=True)
    prior_state = returned_prefix.reshape(block_state.shape)
    inter = jnp.einsum(
        "thd,hde->the", queries.astype(jnp.float32), prior_state, precision=lax.Precision.HIGHEST
    )
    attended = local_part + jnp.exp(cumulative)[:, :, None] * inter
    normed = attended * lax.rsqrt(jnp.mean(attended * attended, axis=-1, keepdims=True) + 1e-06)
    normed = normed * attn_gain.reshape(heads, HEAD)
    mixed = (residual.astype(jnp.float32) + normed.reshape(rows, width)).astype(jnp.bfloat16)
    mixed_f = mixed.astype(jnp.float32)
    gained = mixed_f * norm_gain
    router_f = router.astype(jnp.float32)
    squares = lax.psum(jnp.sum(mixed_f * mixed_f, axis=1), "exp")
    inverse = lax.rsqrt(squares / D + 1e-06)
    scaled = gained * inverse[:, None]
    logits = lax.psum(jnp.dot(scaled, router_f, precision=lax.Precision.HIGHEST), "exp")
    tokens_in = scaled.astype(jnp.bfloat16)
    probs = jax.nn.sigmoid(logits)
    chosen = expert_ids[:, :, None] == jnp.arange(EXPERTS, dtype=jnp.int32)[None, None, :]
    selected = jnp.sum(jnp.where(chosen, probs[:, None, :], 0.0), axis=-1)
    gates = selected / jnp.sum(selected, axis=-1, keepdims=True)
    is_held = expert_ids[:, :, None] == jnp.arange(held, dtype=jnp.int32)[None, None, :]
    member = jnp.where(jnp.any(is_held, axis=1), 1.0, 0.0).astype(jnp.float32)
    gate_held = jnp.sum(jnp.where(is_held, gates[:, :, None], 0.0), axis=1)
    order = priority[0]
    earlier = jnp.where(order[None, :] < order[:, None], 1.0, 0.0).astype(jnp.bfloat16)
    rank = jnp.dot(earlier, member.astype(jnp.bfloat16), preferred_element_type=jnp.float32)
    kept = (member > 0.5) & (rank < CAP)
    slot_ids = jnp.arange(CAP).astype(jnp.float32)
    place = kept.T[:, None, :] & (rank.T[:, None, :] == slot_ids[None, :, None])
    place_f = jnp.where(place, 1.0, 0.0).astype(jnp.float32)
    buffer = jnp.einsum(
        "ect,td->ecd", place_f.astype(jnp.bfloat16), tokens_in, preferred_element_type=jnp.float32
    ).astype(jnp.bfloat16)
    arrived = lax.all_to_all(buffer, "exp", split_axis=0, concat_axis=2, tiled=True)[0]
    gathered = lax.all_gather(arrived, "seq", axis=0, tiled=True)
    gate = jnp.dot(gathered, gate_weight[0], preferred_element_type=jnp.float32)
    up = jnp.dot(gathered, up_weight[0], preferred_element_type=jnp.float32)
    hidden = (jax.nn.silu(gate) * up).astype(jnp.bfloat16)
    weight_rows = down_weight[0]
    summed = jnp.dot(
        lax.all_gather(hidden, "seq", axis=1, tiled=True),
        weight_rows,
        preferred_element_type=jnp.float32,
    )
    expert_out = summed.astype(jnp.bfloat16)
    returned = lax.all_to_all(expert_out, "seq", split_axis=0, concat_axis=1, tiled=True)
    regrouped = lax.all_to_all(returned[None], "exp", split_axis=2, concat_axis=0, tiled=True)
    weighted = place_f * gate_held.T[:, None, :]
    combined = jnp.einsum(
        "ect,ecd->td", weighted, regrouped.astype(jnp.float32), precision=lax.Precision.HIGHEST
    )
    return (mixed_f + combined).astype(jnp.bfloat16)


MESH = pl.DeviceIdType.MESH
F32 = jnp.float32
BF16 = jnp.bfloat16


def layer_kernel(
    ns,
    nx,
    group,
    parts,
    residual,
    query,
    key,
    value,
    log_decay,
    attn_gain,
    norm_gain,
    router,
    ids,
    priority,
    gate_hbm,
    up_hbm,
    down_hbm,
    out,
    weights_gate,
    weights_up,
    weights_down,
    padded,
    cum_rows,
    mixed,
    states,
    chain_out,
    chain_in,
    sums_out,
    sums_in,
    slots_out,
    slots_in,
    inverse_out,
    inverse_in,
    total_in,
    hidden_all,
    total_out,
    back_out,
    back_in,
    chunks,
    weight_sems,
    down_sems,
    chain_sems,
    sums_send,
    sums_recv,
    slots_send,
    slots_recv,
    inverse_send,
    inverse_recv,
    hidden_send,
    hidden_recv,
    back_send,
    back_recv,
):
    rows, width = residual.shape
    heads = width // HEAD
    half = width // 2
    ff = gate_hbm.shape[2]
    span = ff // parts
    s = lax.axis_index("seq")
    x = lax.axis_index("exp")

    barrier = pltpu.get_barrier_semaphore()
    peers = [(a, b) for a in range(ns) for b in range(nx) if (a, b) != (0, 0)]

    def peer(a, b):
        return {"seq": lax.rem(s + a, ns), "exp": lax.rem(x + b, nx)}

    for a, b in peers:
        pl.semaphore_signal(barrier, inc=1, device_id=peer(a, b), device_id_type=MESH)

    weight_copies = [[], []]
    for m in range(2):
        for source in range(nx):
            at = pl.ds(source * width + m * half, half)
            weight_copies[m].append(
                [
                    pltpu.make_async_copy(
                        gate_hbm.at[0, at, :], weights_gate.at[at, :], weight_sems.at[0, m, source]
                    ),
                    pltpu.make_async_copy(
                        up_hbm.at[0, at, :], weights_up.at[at, :], weight_sems.at[1, m, source]
                    ),
                ]
            )
    down_copies = [
        [
            pltpu.make_async_copy(
                down_hbm.at[0, pl.ds(i * ff + p * span, span), :],
                weights_down.at[pl.ds((p * ns + i) * span, span), :],
                down_sems.at[p, i],
            )
            for i in range(ns)
        ]
        for p in range(parts)
    ]
    for copies in weight_copies[0] + weight_copies[1] + down_copies:
        for copy in copies:
            copy.start()

    row_at = lax.broadcasted_iota(jnp.int32, (rows, rows), 0)
    lane_at = lax.broadcasted_iota(jnp.int32, (rows, rows), 1)
    id_rows = [ids[i : i + 1, :].astype(F32) for i in range(2)]
    order = jnp.broadcast_to(priority[...].astype(F32), (rows, rows))
    earlier = jnp.where(order.T < order, 1.0, 0.0).astype(BF16)
    expert_rows = -(-nx // 8) * 8
    expert_at = lax.broadcasted_iota(jnp.int32, (expert_rows, rows), 0).astype(F32)
    member = jnp.where((id_rows[0] == expert_at) | (id_rows[1] == expert_at), 1.0, 0.0)
    rank = jnp.dot(member.astype(BF16), earlier, preferred_element_type=F32)
    slot_at = lax.broadcasted_iota(jnp.int32, (CAP, rows), 0).astype(F32)
    rank = jnp.where(member > 0.5, rank, -1.0)
    place = [jnp.where(rank[e : e + 1, :] == slot_at, 1.0, 0.0) for e in range(nx)]
    place_all = jnp.concatenate(place, axis=0)

    padded[...] = jnp.zeros_like(padded)
    padded[:heads, :] = log_decay[...]
    upper = jnp.where(row_at <= lane_at, 1.0, 0.0).astype(F32)
    cumulative = jnp.dot(
        padded[...], upper, precision=lax.Precision.HIGHEST, preferred_element_type=F32
    )
    cum_rows[...] = cumulative
    padded[...] = cumulative.T

    @pl.when(s == 0)
    def _():
        chain_in[...] = jnp.zeros_like(chain_in)

    pl.semaphore_wait(barrier, len(peers))

    def chain_copy(i):
        return pltpu.make_async_remote_copy(
            src_ref=chain_out.at[i],
            dst_ref=chain_in.at[i],
            send_sem=chain_sems.at[0, i],
            recv_sem=chain_sems.at[1, i],
            device_id={"seq": lax.rem(s + 1, ns)},
            device_id_type=MESH,
        )

    cluster = 2 * group
    for first in range(0, heads, cluster):
        for head in range(first, first + cluster):
            at = slice(head * HEAD, (head + 1) * HEAD)
            col = padded[:, head : head + 1]
            to_end = jnp.exp(col[rows - 1 : rows, :] - col)
            keyed = (key[:, at].astype(F32) * to_end).astype(BF16)
            state = lax.dot_general(
                keyed, value[:, at], (((0,), (0,)), ((), ())), preferred_element_type=F32
            )
            states[head] = state
            chain_out[head] = state.astype(BF16)

        @pl.when(s == 0)
        def _():
            for head in range(first, first + cluster):
                chain_copy(head).start()

    causal = row_at >= lane_at

    def attend(i, carry):
        cols = []
        for g in range(group):
            head = i * group + g
            cols.append(
                jnp.sum(jnp.where(lane_at == head, padded[...], 0.0), axis=1, keepdims=True)
            )

        @pl.when(s > 0)
        def _():
            for g in range(group):
                head = i * group + g
                chain_copy(head).wait_recv()

                @pl.when(s < ns - 1)
                def _():
                    decay = jnp.exp(cols[g][rows - 1 : rows, :])
                    prior = chain_in[head].astype(F32)
                    chain_out[head] = (decay * prior + states[head]).astype(BF16)
                    chain_copy(head).start()

        for g in range(group):
            head = i * group + g
            at = pl.ds(pl.multiple_of(head * HEAD, HEAD), HEAD)
            col, row = cols[g], cum_rows[pl.ds(head, 1), :]
            q, k, v = query[:, at], key[:, at], value[:, at]
            scores = lax.dot_general(q, k, (((1,), (1,)), ((), ())), preferred_element_type=F32)
            spread = jnp.where(causal, col - row, 0.0)
            weights = jnp.where(causal, scores * jnp.exp(spread), 0.0).astype(BF16)
            local = jnp.dot(weights, v, preferred_element_type=F32)
            inter = jnp.dot(q, chain_in[head], preferred_element_type=F32)
            attended = local + jnp.exp(col) * inter
            mean = jnp.sum(attended * attended, axis=1, keepdims=True) / HEAD
            normed = attended * lax.rsqrt(mean + 1e-06) * attn_gain[pl.ds(head, 1), :]
            mixed[:, at] = (residual[:, at].astype(F32) + normed).astype(BF16)
        return carry

    def slots_copy(m, a, b):
        return pltpu.make_async_remote_copy(
            src_ref=slots_out.at[m, lax.rem(x + b, nx)],
            dst_ref=slots_in.at[m, s, x],
            send_sem=slots_send.at[m, a, b],
            recv_sem=slots_recv.at[m, s, x],
            device_id=peer(a, b),
            device_id_type=MESH,
        )

    def slots_arrive(m, block, source):
        return pltpu.make_async_remote_copy(
            src_ref=slots_out.at[m, 0],
            dst_ref=slots_in.at[m, block, source],
            send_sem=slots_send.at[m, 0, 0],
            recv_sem=slots_recv.at[m, block, source],
            device_id=peer(1, 1),
            device_id_type=MESH,
        )

    place_b = place_all.astype(BF16)
    steps = heads // group // 2
    heads_half = heads // 2
    quarter = half // 2
    logits = jnp.zeros((rows, router.shape[0]), F32)
    squares = jnp.zeros((rows, 1), F32)
    for m in range(2):
        lax.fori_loop(m * steps, (m + 1) * steps, attend, 0)
        gained = []
        for head in range(m * heads_half, (m + 1) * heads_half):
            mixed_f = mixed[:, head * HEAD : (head + 1) * HEAD].astype(F32)
            squares = squares + jnp.sum(mixed_f * mixed_f, axis=1, keepdims=True)
            gained.append(mixed_f * norm_gain[head : head + 1, :])
        gained = jnp.concatenate(gained, axis=1)
        tokens = gained.astype(BF16)
        picked = jnp.dot(place_b, tokens, preferred_element_type=F32)
        for e in range(nx):
            at = slice(e * CAP, (e + 1) * CAP)
            slots_out[m, e] = jnp.concatenate(
                [picked[at, :quarter], picked[at, quarter:]], axis=0
            ).astype(BF16)
        slots_in[m, s, x] = slots_out[m, x]
        for a, b in peers:
            slots_copy(m, a, b).start()
        rest = (gained - tokens.astype(F32)).astype(BF16)
        router_half = router[:, m * half : (m + 1) * half]
        for part in (tokens, rest):
            logits = logits + lax.dot_general(
                part, router_half, (((1,), (1,)), ((), ())), preferred_element_type=F32
            )

    padded[...] = jnp.zeros_like(padded)
    padded[:, : router.shape[0]] = logits
    logits_t = padded[...].T
    expert_row = row_at.astype(F32)
    chosen = [
        jnp.sum(jnp.where(expert_row == r, logits_t, 0.0), axis=0, keepdims=True) for r in id_rows
    ]
    squares_t = jnp.broadcast_to(squares, (rows, rows)).T[0:1, :]
    sums = jnp.concatenate([chosen[0], chosen[1], squares_t] + [squares_t] * 5, axis=0)
    sums_out[...] = sums
    sums_in[x] = sums

    def sums_copy(b):
        return pltpu.make_async_remote_copy(
            src_ref=sums_out,
            dst_ref=sums_in.at[x],
            send_sem=sums_send.at[b],
            recv_sem=sums_recv.at[x],
            device_id=peer(0, b),
            device_id_type=MESH,
        )

    def sums_arrive(b):
        source = lax.rem(x + b, nx)
        return pltpu.make_async_remote_copy(
            src_ref=sums_out,
            dst_ref=sums_in.at[source],
            send_sem=sums_send.at[b],
            recv_sem=sums_recv.at[source],
            device_id=peer(0, b),
            device_id_type=MESH,
        )

    for b in range(1, nx):
        sums_copy(b).start()

    def slots_wait(m):
        for a, b in peers:
            slots_arrive(m, lax.rem(s + a, ns), lax.rem(x + b, nx)).wait_recv()

    def chunk_of(m, source):
        arrived = [slots_in[m, i, source].astype(F32) for i in range(ns)]
        return jnp.concatenate(
            [
                jnp.concatenate([r[h * CAP : (h + 1) * CAP] for r in arrived], axis=0)
                for h in range(2)
            ],
            axis=1,
        ).astype(BF16)

    def product_of(m, source, chunk, at):
        start = source * width + m * half
        return [
            jnp.dot(chunk, w[start : start + half, at], preferred_element_type=F32)
            for w in (weights_gate, weights_up)
        ]

    slots_wait(0)
    for source in range(nx):
        for copy in weight_copies[0][source]:
            copy.wait()
        products = product_of(0, source, chunk_of(0, source), slice(0, ff))
        for j in range(2):
            at = slice(j * ff, (j + 1) * ff)
            total_in[:, at] = products[j] if source == 0 else total_in[:, at] + products[j]

    for b in range(1, nx):
        sums_arrive(b).wait_recv()
    added = sums_in[0]
    for b in range(1, nx):
        added = added + sums_in[b]
    inverse = lax.rsqrt(added[2:3, :] / (width * nx) + 1e-06)
    slot_inverse = jnp.sum(place_all * inverse, axis=1, keepdims=True)
    slot_inverse = jnp.broadcast_to(slot_inverse, place_all.shape)
    for e in range(nx):
        inverse_out[e] = slot_inverse[e * CAP : (e + 1) * CAP, :]
    inverse_in[s] = inverse_out[x]

    def inverse_copy(a):
        return pltpu.make_async_remote_copy(
            src_ref=inverse_out.at[x],
            dst_ref=inverse_in.at[s],
            send_sem=inverse_send.at[a],
            recv_sem=inverse_recv.at[s],
            device_id=peer(a, 0),
            device_id_type=MESH,
        )

    def inverse_arrive(a):
        source = lax.rem(s + a, ns)
        return pltpu.make_async_remote_copy(
            src_ref=inverse_out.at[x],
            dst_ref=inverse_in.at[source],
            send_sem=inverse_send.at[a],
            recv_sem=inverse_recv.at[source],
            device_id=peer(a, 0),
            device_id_type=MESH,
        )

    for a in range(1, ns):
        inverse_copy(a).start()

    slots_wait(1)
    for source in range(nx):
        chunks[source] = chunk_of(1, source)
    for a in range(1, ns):
        inverse_arrive(a).wait_recv()
    scale = jnp.concatenate([inverse_in[i] for i in range(ns)], axis=0)[:, :1]

    def hidden_copy(p, a):
        return pltpu.make_async_remote_copy(
            src_ref=hidden_all.at[s, p],
            dst_ref=hidden_all.at[s, p],
            send_sem=hidden_send.at[p, a],
            recv_sem=hidden_recv.at[p, s],
            device_id=peer(a, 0),
            device_id_type=MESH,
        )

    def hidden_arrive(p, a):
        source = lax.rem(s + a, ns)
        return pltpu.make_async_remote_copy(
            src_ref=hidden_all.at[s, p],
            dst_ref=hidden_all.at[source, p],
            send_sem=hidden_send.at[p, a],
            recv_sem=hidden_recv.at[p, source],
            device_id=peer(a, 0),
            device_id_type=MESH,
        )

    for p in range(parts):
        gate = total_in[:, p * span : (p + 1) * span]
        up = total_in[:, ff + p * span : ff + (p + 1) * span]
        for source in range(nx):
            if p == 0:
                for copy in weight_copies[1][source]:
                    copy.wait()
            products = product_of(1, source, chunks[source], slice(p * span, (p + 1) * span))
            gate, up = gate + products[0], up + products[1]
        hidden_all[s, p] = (jax.nn.silu(gate * scale) * (up * scale)).astype(BF16)
        for a in range(1, ns):
            hidden_copy(p, a).start()

    probs = [jax.nn.sigmoid(added[i : i + 1, :] * inverse) for i in range(2)]
    gates = [r / (probs[0] + probs[1]) for r in probs]
    weighted = jnp.concatenate(
        [
            place[e]
            * (
                jnp.where(id_rows[0] == e, gates[0], 0.0)
                + jnp.where(id_rows[1] == e, gates[1], 0.0)
            )
            for e in range(nx)
        ],
        axis=0,
    )
    slots = nx * CAP
    padded[...] = jnp.zeros_like(padded)
    padded[:slots, :] = weighted
    weighted = padded[...].T[:, :slots]
    weighted_high = weighted.astype(BF16)
    weighted_low = (weighted - weighted_high.astype(F32)).astype(BF16)

    def down_product(p, at):
        hidden = jnp.concatenate([hidden_all[i, p] for i in range(ns)], axis=1)
        return jnp.dot(
            hidden,
            weights_down[p * ns * span : (p + 1) * ns * span, at],
            preferred_element_type=F32,
        )

    def back_copy(h, block):
        return pltpu.make_async_remote_copy(
            src_ref=back_out.at[h, block],
            dst_ref=back_in.at[h, x],
            send_sem=back_send.at[h, block],
            recv_sem=back_recv.at[h, x],
            device_id={"seq": block, "exp": s},
            device_id_type=MESH,
        )

    def back_arrive(h, e):
        return pltpu.make_async_remote_copy(
            src_ref=back_out.at[h, 0],
            dst_ref=back_in.at[h, e],
            send_sem=back_send.at[h, 0],
            recv_sem=back_recv.at[h, e],
            device_id={"seq": x, "exp": e},
            device_id_type=MESH,
        )

    for p in range(parts):
        for a in range(1, ns):
            hidden_arrive(p, a).wait_recv()
        for copy in down_copies[p]:
            copy.wait()
        if p < parts - 1:
            product = down_product(p, slice(0, width))
            total_out[...] = product if p == 0 else total_out[...] + product
    for h in range(2):
        at = slice(h * half, (h + 1) * half)
        total = down_product(parts - 1, at)
        if parts > 1:
            total = total + total_out[:, at]
        for b in range(ns):
            of = slice(b * CAP, (b + 1) * CAP)
            back_out[h, b] = jnp.concatenate(
                [total[of, :quarter], total[of, quarter:]], axis=0
            ).astype(BF16)
        for a in range(1, ns):
            back_copy(h, lax.rem(s + a, ns)).start()

        @pl.when(x != s)
        def _():
            back_copy(h, s).start()

        @pl.when(x == s)
        def _():
            back_in[h, x] = back_out[h, s]

    for h in range(2):
        for b in range(1, nx):
            back_arrive(h, lax.rem(x + b, nx)).wait_recv()

        @pl.when(x != s)
        def _():
            back_arrive(h, x).wait_recv()

        returned = [back_in[h, e].astype(F32) for e in range(nx)]
        expert_out = jnp.concatenate(
            [
                jnp.concatenate([r[j * CAP : (j + 1) * CAP] for r in returned], axis=0)
                for j in range(2)
            ],
            axis=1,
        ).astype(BF16)
        combined = jnp.dot(weighted_high, expert_out, preferred_element_type=F32) + jnp.dot(
            weighted_low, expert_out, preferred_element_type=F32
        )
        at = slice(h * half, (h + 1) * half)
        out[:, at] = (mixed[:, at].astype(F32) + combined).astype(BF16)

    @pl.when(s < ns - 1)
    def _():
        for head in range(heads):
            chain_copy(head).wait_send()

    for m in range(2):
        for a, b in peers:
            slots_copy(m, a, b).wait_send()
    for b in range(1, nx):
        sums_copy(b).wait_send()
    for a in range(1, ns):
        inverse_copy(a).wait_send()
        for p in range(parts):
            hidden_copy(p, a).wait_send()
    for h in range(2):
        for a in range(1, ns):
            back_copy(h, lax.rem(s + a, ns)).wait_send()

        @pl.when(x != s)
        def _():
            back_copy(h, s).wait_send()


def fused_body(
    residual,
    query_rows,
    key_rows,
    value_rows,
    log_decay,
    attn_gain,
    norm_gain,
    router,
    expert_ids,
    priority,
    gate_weight,
    up_weight,
    down_weight,
):
    ns, nx = lax.axis_size("seq"), lax.axis_size("exp")
    rows, width = residual.shape
    heads = width // HEAD
    group = 2 if heads % 4 == 0 else 1
    depth, ff = gate_weight.shape[1:]
    half = width // 2
    parts = next(n for n in (3, 2, 1) if ff % (n * HEAD) == 0)
    dma = pltpu.SemaphoreType.DMA
    in_vmem = pl.BlockSpec(memory_space=pltpu.VMEM)
    in_place = pl.BlockSpec(memory_space=pl.ANY)
    return pl.pallas_call(
        functools.partial(layer_kernel, ns, nx, group, parts),
        out_shape=jax.ShapeDtypeStruct((rows, width), BF16),
        in_specs=[in_vmem] * 10 + [in_place] * 3,
        out_specs=in_vmem,
        scratch_shapes=[
            pltpu.VMEM((depth, ff), BF16),
            pltpu.VMEM((depth, ff), BF16),
            pltpu.VMEM(down_weight.shape[1:], BF16),
            pltpu.VMEM((rows, rows), F32),
            pltpu.VMEM((rows, rows), F32),
            pltpu.VMEM((rows, width), BF16),
            pltpu.VMEM((heads, HEAD, HEAD), F32),
            pltpu.VMEM((heads, HEAD, HEAD), BF16),
            pltpu.VMEM((heads, HEAD, HEAD), BF16),
            pltpu.VMEM((8, rows), F32),
            pltpu.VMEM((nx, 8, rows), F32),
            pltpu.VMEM((2, nx, 2 * CAP, half // 2), BF16),
            pltpu.VMEM((2, ns, nx, 2 * CAP, half // 2), BF16),
            pltpu.VMEM((nx, CAP, rows), F32),
            pltpu.VMEM((ns, CAP, rows), F32),
            pltpu.VMEM((ns * CAP, 2 * ff), F32),
            pltpu.VMEM((ns, parts, ns * CAP, ff // parts), BF16),
            pltpu.VMEM((ns * CAP, width), F32),
            pltpu.VMEM((2, ns, 2 * CAP, half // 2), BF16),
            pltpu.VMEM((2, nx, 2 * CAP, half // 2), BF16),
            pltpu.VMEM((nx, ns * CAP, half), BF16),
            dma((2, 2, nx)),
            dma((parts, ns)),
            dma((2, heads)),
            dma((nx,)),
            dma((nx,)),
            dma((2, ns, nx)),
            dma((2, ns, nx)),
            dma((ns,)),
            dma((ns,)),
            dma((parts, ns)),
            dma((parts, ns)),
            dma((2, ns)),
            dma((2, nx)),
        ],
        compiler_params=pltpu.CompilerParams(
            collective_id=0, has_side_effects=True, vmem_limit_bytes=60 * 1024 * 1024
        ),
        cost_estimate=pl.CostEstimate(
            flops=6 * ns * CAP * depth * ff,
            bytes_accessed=6 * depth * ff,
            transcendentals=heads * rows * rows,
        ),
    )(
        residual,
        query_rows,
        key_rows,
        value_rows,
        log_decay.T,
        attn_gain.reshape(heads, HEAD),
        norm_gain.reshape(heads, HEAD),
        router.T,
        expert_ids.T,
        priority,
        gate_weight,
        up_weight,
        down_weight,
    )


def body(*args):
    rows, width = args[0].shape
    ff, columns = args[10].shape[2], args[12].shape[2]
    aligned = (
        rows == HEAD
        and ff % HEAD == 0
        and width % (4 * HEAD) == 0
        and columns == width
        and args[10].shape[0] == 1
        and lax.axis_size("seq") == lax.axis_size("exp")
    )
    return (fused_body if aligned else plain_body)(*args)


def solution(mesh):
    return jax.shard_map(
        body,
        mesh=mesh,
        in_specs=(
            P(("groups", "seq"), "exp"),
            P(("groups", "seq"), "exp"),
            P(("groups", "seq"), "exp"),
            P(("groups", "seq"), "exp"),
            P(("groups", "seq"), "exp"),
            P("exp"),
            P("exp"),
            P("exp", None),
            P(("groups", "seq"), None),
            P(("groups", "seq"), None),
            P("exp", None, "seq"),
            P("exp", None, "seq"),
            P("exp", None, "seq"),
        ),
        out_specs=P(("groups", "seq"), "exp"),
        check_vma=False,
    )
```

```python
import functools

import jax
import jax.numpy as jnp
from jax import lax
from jax.experimental import pallas as pl
from jax.experimental.pallas import tpu as pltpu
from jax.sharding import PartitionSpec as P

D = 6144
HEAD = 128
EXPERTS = 32
CAP = 8


def link_states(earlier, later):
    return (earlier[0] * later[0], later[0] * earlier[1] + later[1])


def plain_body(
    residual,
    query_rows,
    key_rows,
    value_rows,
    log_decay,
    attn_gain,
    norm_gain,
    router,
    expert_ids,
    priority,
    gate_weight,
    up_weight,
    down_weight,
):
    rows = residual.shape[0]
    width = residual.shape[1]
    heads = width // HEAD
    held = lax.axis_size("exp")
    queries = query_rows.reshape(rows, heads, HEAD)
    keys_local = key_rows.reshape(rows, heads, HEAD)
    values = value_rows.reshape(rows, heads, HEAD)
    cumulative = jnp.cumsum(log_decay, axis=0)
    scores = jnp.einsum("thd,shd->hts", queries, keys_local, preferred_element_type=jnp.float32)
    causal = (jnp.arange(rows)[:, None] >= jnp.arange(rows)[None, :])[None]
    spread = cumulative.T[:, :, None] - cumulative.T[:, None, :]
    weights = jnp.where(causal, scores * jnp.exp(jnp.where(causal, spread, 0.0)), 0.0).astype(
        jnp.bfloat16
    )
    local_part = jnp.einsum("hts,shd->thd", weights, values, preferred_element_type=jnp.float32)
    to_end = jnp.exp(cumulative[-1][None, :] - cumulative)
    keyed = (keys_local.astype(jnp.float32) * to_end[:, :, None]).astype(jnp.bfloat16)
    block_state = jnp.einsum("thd,the->hde", keyed, values, preferred_element_type=jnp.float32)
    block_decay = jnp.exp(cumulative[-1])
    seq_count = lax.axis_size("seq")
    share_size = block_state.size // seq_count
    flat_state = block_state.reshape(seq_count, share_size)
    tiled_decay = jnp.broadcast_to(block_decay[None, :], (seq_count, heads))
    arrived_state, arrived_decay = (
        lax.all_to_all(flat_state, "seq", split_axis=0, concat_axis=0, tiled=True),
        lax.all_to_all(tiled_decay, "seq", split_axis=0, concat_axis=0, tiled=True),
    )
    position = lax.axis_index("seq") * share_size + jnp.arange(share_size, dtype=jnp.int32)
    owner_head = position // (HEAD * HEAD)
    selector = jnp.where(
        owner_head[None, :] == jnp.arange(heads, dtype=jnp.int32)[:, None], 1.0, 0.0
    ).astype(jnp.float32)
    element_decay = jnp.dot(arrived_decay, selector, precision=lax.Precision.HIGHEST)
    inclusive = lax.associative_scan(link_states, (element_decay, arrived_state), axis=0)[1]
    exclusive = jnp.concatenate([jnp.zeros((1, share_size), jnp.float32), inclusive[:-1]], axis=0)
    returned_prefix = lax.all_to_all(exclusive, "seq", split_axis=0, concat_axis=0, tiled=True)
    prior_state = returned_prefix.reshape(block_state.shape)
    inter = jnp.einsum(
        "thd,hde->the", queries.astype(jnp.float32), prior_state, precision=lax.Precision.HIGHEST
    )
    attended = local_part + jnp.exp(cumulative)[:, :, None] * inter
    normed = attended * lax.rsqrt(jnp.mean(attended * attended, axis=-1, keepdims=True) + 1e-06)
    normed = normed * attn_gain.reshape(heads, HEAD)
    mixed = (residual.astype(jnp.float32) + normed.reshape(rows, width)).astype(jnp.bfloat16)
    mixed_f = mixed.astype(jnp.float32)
    gained = mixed_f * norm_gain
    router_f = router.astype(jnp.float32)
    squares = lax.psum(jnp.sum(mixed_f * mixed_f, axis=1), "exp")
    inverse = lax.rsqrt(squares / D + 1e-06)
    scaled = gained * inverse[:, None]
    logits = lax.psum(jnp.dot(scaled, router_f, precision=lax.Precision.HIGHEST), "exp")
    tokens_in = scaled.astype(jnp.bfloat16)
    probs = jax.nn.sigmoid(logits)
    chosen = expert_ids[:, :, None] == jnp.arange(EXPERTS, dtype=jnp.int32)[None, None, :]
    selected = jnp.sum(jnp.where(chosen, probs[:, None, :], 0.0), axis=-1)
    gates = selected / jnp.sum(selected, axis=-1, keepdims=True)
    is_held = expert_ids[:, :, None] == jnp.arange(held, dtype=jnp.int32)[None, None, :]
    member = jnp.where(jnp.any(is_held, axis=1), 1.0, 0.0).astype(jnp.float32)
    gate_held = jnp.sum(jnp.where(is_held, gates[:, :, None], 0.0), axis=1)
    order = priority[0]
    earlier = jnp.where(order[None, :] < order[:, None], 1.0, 0.0).astype(jnp.bfloat16)
    rank = jnp.dot(earlier, member.astype(jnp.bfloat16), preferred_element_type=jnp.float32)
    kept = (member > 0.5) & (rank < CAP)
    slot_ids = jnp.arange(CAP).astype(jnp.float32)
    place = kept.T[:, None, :] & (rank.T[:, None, :] == slot_ids[None, :, None])
    place_f = jnp.where(place, 1.0, 0.0).astype(jnp.float32)
    buffer = jnp.einsum(
        "ect,td->ecd", place_f.astype(jnp.bfloat16), tokens_in, preferred_element_type=jnp.float32
    ).astype(jnp.bfloat16)
    arrived = lax.all_to_all(buffer, "exp", split_axis=0, concat_axis=2, tiled=True)[0]
    gathered = lax.all_gather(arrived, "seq", axis=0, tiled=True)
    gate = jnp.dot(gathered, gate_weight[0], preferred_element_type=jnp.float32)
    up = jnp.dot(gathered, up_weight[0], preferred_element_type=jnp.float32)
    hidden = (jax.nn.silu(gate) * up).astype(jnp.bfloat16)
    weight_rows = down_weight[0]
    summed = jnp.dot(
        lax.all_gather(hidden, "seq", axis=1, tiled=True),
        weight_rows,
        preferred_element_type=jnp.float32,
    )
    expert_out = summed.astype(jnp.bfloat16)
    returned = lax.all_to_all(expert_out, "seq", split_axis=0, concat_axis=1, tiled=True)
    regrouped = lax.all_to_all(returned[None], "exp", split_axis=2, concat_axis=0, tiled=True)
    weighted = place_f * gate_held.T[:, None, :]
    combined = jnp.einsum(
        "ect,ecd->td", weighted, regrouped.astype(jnp.float32), precision=lax.Precision.HIGHEST
    )
    return (mixed_f + combined).astype(jnp.bfloat16)


MESH = pl.DeviceIdType.MESH
F32 = jnp.float32
INPUTS = 10
BF16 = jnp.bfloat16


def layer_kernel(
    ns,
    nx,
    group,
    parts,
    *refs,
):
    arrays, refs = refs[:INPUTS], refs[INPUTS:]
    (gate_hbm, up_hbm, down_hbm, out_hbm), refs = refs[:4], refs[4:]
    local, refs = refs[:INPUTS], refs[INPUTS:]
    (residual, query, key, value, log_decay, attn_gain, norm_gain, router, ids, priority) = local
    (
    out,
    input_sems,
    out_sems,
    weights_in,
    weights_down,
    padded,
    cum_rows,
    mixed,
    states,
    chain_out,
    chain_in,
    sums_out,
    sums_in,
    slots_out,
    slots_in,
    inverse_out,
    inverse_in,
    total_in,
    hidden_all,
    total_out,
    back_out,
    back_in,
    chunks,
    weight_sems,
    down_sems,
    chain_sems,
    sums_send,
    sums_recv,
    slots_send,
    slots_recv,
    inverse_send,
    inverse_recv,
    hidden_send,
    hidden_recv,
    back_send,
    back_recv,
    ) = refs
    rows, width = residual.shape
    heads = width // HEAD
    half = width // 2
    ff = gate_hbm.shape[3]
    span = ff // parts
    s = lax.axis_index("seq")
    x = lax.axis_index("exp")

    barrier = pltpu.get_barrier_semaphore()
    peers = [(a, b) for a in range(ns) for b in range(nx) if (a, b) != (0, 0)]

    def peer(a, b):
        return {"seq": lax.rem(s + a, ns), "exp": lax.rem(x + b, nx)}

    for a, b in peers:
        pl.semaphore_signal(barrier, inc=1, device_id=peer(a, b), device_id_type=MESH)

    input_copies = {}
    for i in (4, 8, 9, 2, 3, 1, 0, 5, 6, 7):
        input_copies[i] = pltpu.make_async_copy(arrays[i], local[i], input_sems.at[i])
        input_copies[i].start()

    def ready(*which):
        for i in which:
            input_copies[i].wait()

    weight_copies = [
        [
            pltpu.make_async_copy(
                source.at[:, m, :, pl.ds(p * span, span)],
                weights_in.at[:, m, :, pl.ds((2 * p + j) * span, span)],
                weight_sems.at[m, p, j],
            )
            for p in range(parts)
            for j, source in enumerate((gate_hbm, up_hbm))
        ]
        for m in range(2)
    ]
    down_copies = [
        [pltpu.make_async_copy(down_hbm.at[:, p], weights_down.at[p], down_sems.at[p])]
        for p in range(parts)
    ]
    for copies in weight_copies + down_copies:
        for copy in copies:
            copy.start()

    ready(4, 8, 9)
    row_at = lax.broadcasted_iota(jnp.int32, (rows, rows), 0)
    lane_at = lax.broadcasted_iota(jnp.int32, (rows, rows), 1)
    id_rows = [ids[i : i + 1, :].astype(F32) for i in range(2)]
    order = jnp.broadcast_to(priority[...].astype(F32), (rows, rows))
    earlier = jnp.where(order.T < order, 1.0, 0.0).astype(BF16)
    expert_rows = -(-nx // 8) * 8
    expert_at = lax.broadcasted_iota(jnp.int32, (expert_rows, rows), 0).astype(F32)
    member = jnp.where((id_rows[0] == expert_at) | (id_rows[1] == expert_at), 1.0, 0.0)
    rank = jnp.dot(member.astype(BF16), earlier, preferred_element_type=F32)
    slot_at = lax.broadcasted_iota(jnp.int32, (CAP, rows), 0).astype(F32)
    rank = jnp.where(member > 0.5, rank, -1.0)
    place = [jnp.where(rank[e : e + 1, :] == slot_at, 1.0, 0.0) for e in range(nx)]
    place_all = jnp.concatenate(place, axis=0)

    padded[...] = jnp.zeros_like(padded)
    padded[:heads, :] = log_decay[...]
    upper = jnp.where(row_at <= lane_at, 1.0, 0.0).astype(F32)
    cumulative = jnp.dot(
        padded[...], upper, precision=lax.Precision.HIGHEST, preferred_element_type=F32
    )
    cum_rows[...] = cumulative
    padded[...] = cumulative.T

    @pl.when(s == 0)
    def _():
        chain_in[...] = jnp.zeros_like(chain_in)

    pl.semaphore_wait(barrier, len(peers))

    def chain_copy(i):
        return pltpu.make_async_remote_copy(
            src_ref=chain_out.at[i],
            dst_ref=chain_in.at[i],
            send_sem=chain_sems.at[0, i],
            recv_sem=chain_sems.at[1, i],
            device_id={"seq": lax.rem(s + 1, ns)},
            device_id_type=MESH,
        )

    ready(2, 3)
    cluster = 2 * group
    for first in range(0, heads, cluster):
        for head in range(first, first + cluster):
            at = slice(head * HEAD, (head + 1) * HEAD)
            col = padded[:, head : head + 1]
            to_end = jnp.exp(col[rows - 1 : rows, :] - col)
            keyed = (key[:, at].astype(F32) * to_end).astype(BF16)
            state = lax.dot_general(
                keyed, value[:, at], (((0,), (0,)), ((), ())), preferred_element_type=F32
            )
            states[head] = state
            chain_out[head] = state.astype(BF16)

        @pl.when(s == 0)
        def _():
            for head in range(first, first + cluster):
                chain_copy(head).start()

    causal = row_at >= lane_at

    def attend(i, carry):
        cols = []
        for g in range(group):
            head = i * group + g
            cols.append(
                jnp.sum(jnp.where(lane_at == head, padded[...], 0.0), axis=1, keepdims=True)
            )

        @pl.when(s > 0)
        def _():
            for g in range(group):
                head = i * group + g
                chain_copy(head).wait_recv()

                @pl.when(s < ns - 1)
                def _():
                    decay = jnp.exp(cols[g][rows - 1 : rows, :])
                    prior = chain_in[head].astype(F32)
                    chain_out[head] = (decay * prior + states[head]).astype(BF16)
                    chain_copy(head).start()

        for g in range(group):
            head = i * group + g
            at = pl.ds(pl.multiple_of(head * HEAD, HEAD), HEAD)
            col, row = cols[g], cum_rows[pl.ds(head, 1), :]
            q, k, v = query[:, at], key[:, at], value[:, at]
            scores = lax.dot_general(q, k, (((1,), (1,)), ((), ())), preferred_element_type=F32)
            spread = jnp.where(causal, col - row, 0.0)
            weights = jnp.where(causal, scores * jnp.exp(spread), 0.0).astype(BF16)
            nearby = jnp.dot(weights, v, preferred_element_type=F32)
            inter = jnp.dot(q, chain_in[head], preferred_element_type=F32)
            attended = nearby + jnp.exp(col) * inter
            mean = jnp.sum(attended * attended, axis=1, keepdims=True) / HEAD
            normed = attended * lax.rsqrt(mean + 1e-06) * attn_gain[pl.ds(head, 1), :]
            mixed[:, at] = (residual[:, at].astype(F32) + normed).astype(BF16)
        return carry

    def slots_copy(m, a, b):
        return pltpu.make_async_remote_copy(
            src_ref=slots_out.at[m, lax.rem(x + b, nx)],
            dst_ref=slots_in.at[m, s, x],
            send_sem=slots_send.at[m, a, b],
            recv_sem=slots_recv.at[m, s, x],
            device_id=peer(a, b),
            device_id_type=MESH,
        )

    def slots_arrive(m, block, source):
        return pltpu.make_async_remote_copy(
            src_ref=slots_out.at[m, 0],
            dst_ref=slots_in.at[m, block, source],
            send_sem=slots_send.at[m, 0, 0],
            recv_sem=slots_recv.at[m, block, source],
            device_id=peer(1, 1),
            device_id_type=MESH,
        )

    ready(1, 0, 5, 6, 7)
    place_b = place_all.astype(BF16)
    steps = heads // group // 2
    heads_half = heads // 2
    quarter = half // 2
    logits = jnp.zeros((rows, router.shape[0]), F32)
    squares = jnp.zeros((rows, 1), F32)
    for m in range(2):
        lax.fori_loop(m * steps, (m + 1) * steps, attend, 0)
        gained = []
        for head in range(m * heads_half, (m + 1) * heads_half):
            mixed_f = mixed[:, head * HEAD : (head + 1) * HEAD].astype(F32)
            squares = squares + jnp.sum(mixed_f * mixed_f, axis=1, keepdims=True)
            gained.append(mixed_f * norm_gain[head : head + 1, :])
        gained = jnp.concatenate(gained, axis=1)
        tokens = gained.astype(BF16)
        picked = jnp.dot(place_b, tokens, preferred_element_type=F32)
        for e in range(nx):
            at = slice(e * CAP, (e + 1) * CAP)
            slots_out[m, e] = jnp.concatenate(
                [picked[at, :quarter], picked[at, quarter:]], axis=0
            ).astype(BF16)
        slots_in[m, s, x] = slots_out[m, x]
        for a, b in peers:
            slots_copy(m, a, b).start()
        rest = (gained - tokens.astype(F32)).astype(BF16)
        router_half = router[:, m * half : (m + 1) * half]
        for part in (tokens, rest):
            logits = logits + lax.dot_general(
                part, router_half, (((1,), (1,)), ((), ())), preferred_element_type=F32
            )

    padded[...] = jnp.zeros_like(padded)
    padded[:, : router.shape[0]] = logits
    logits_t = padded[...].T
    expert_row = row_at.astype(F32)
    chosen = [
        jnp.sum(jnp.where(expert_row == r, logits_t, 0.0), axis=0, keepdims=True) for r in id_rows
    ]
    squares_t = jnp.broadcast_to(squares, (rows, rows)).T[0:1, :]
    sums = jnp.concatenate([chosen[0], chosen[1], squares_t] + [squares_t] * 5, axis=0)
    sums_out[...] = sums
    sums_in[x] = sums

    def sums_copy(b):
        return pltpu.make_async_remote_copy(
            src_ref=sums_out,
            dst_ref=sums_in.at[x],
            send_sem=sums_send.at[b],
            recv_sem=sums_recv.at[x],
            device_id=peer(0, b),
            device_id_type=MESH,
        )

    def sums_arrive(b):
        source = lax.rem(x + b, nx)
        return pltpu.make_async_remote_copy(
            src_ref=sums_out,
            dst_ref=sums_in.at[source],
            send_sem=sums_send.at[b],
            recv_sem=sums_recv.at[source],
            device_id=peer(0, b),
            device_id_type=MESH,
        )

    for b in range(1, nx):
        sums_copy(b).start()

    def slots_wait(m):
        for a, b in peers:
            slots_arrive(m, lax.rem(s + a, ns), lax.rem(x + b, nx)).wait_recv()

    def chunk_of(m, source):
        arrived = [slots_in[m, i, source].astype(F32) for i in range(ns)]
        return jnp.concatenate(
            [
                jnp.concatenate([r[h * CAP : (h + 1) * CAP] for r in arrived], axis=0)
                for h in range(2)
            ],
            axis=1,
        ).astype(BF16)

    def product_of(m, source, chunk, at):
        return jnp.dot(chunk, weights_in[source, m, :, at], preferred_element_type=F32)

    slots_wait(0)
    for copy in weight_copies[0]:
        copy.wait()
    for source in range(nx):
        product = product_of(0, source, chunk_of(0, source), slice(0, 2 * ff))
        total_in[...] = product if source == 0 else total_in[...] + product

    for b in range(1, nx):
        sums_arrive(b).wait_recv()
    added = sums_in[0]
    for b in range(1, nx):
        added = added + sums_in[b]
    inverse = lax.rsqrt(added[2:3, :] / (width * nx) + 1e-06)
    slot_inverse = jnp.sum(place_all * inverse, axis=1, keepdims=True)
    slot_inverse = jnp.broadcast_to(slot_inverse, place_all.shape)
    for e in range(nx):
        inverse_out[e] = slot_inverse[e * CAP : (e + 1) * CAP, :]
    inverse_in[s] = inverse_out[x]

    def inverse_copy(a):
        return pltpu.make_async_remote_copy(
            src_ref=inverse_out.at[x],
            dst_ref=inverse_in.at[s],
            send_sem=inverse_send.at[a],
            recv_sem=inverse_recv.at[s],
            device_id=peer(a, 0),
            device_id_type=MESH,
        )

    def inverse_arrive(a):
        source = lax.rem(s + a, ns)
        return pltpu.make_async_remote_copy(
            src_ref=inverse_out.at[x],
            dst_ref=inverse_in.at[source],
            send_sem=inverse_send.at[a],
            recv_sem=inverse_recv.at[source],
            device_id=peer(a, 0),
            device_id_type=MESH,
        )

    for a in range(1, ns):
        inverse_copy(a).start()

    slots_wait(1)
    for source in range(nx):
        chunks[source] = chunk_of(1, source)
    for a in range(1, ns):
        inverse_arrive(a).wait_recv()
    scale = jnp.concatenate([inverse_in[i] for i in range(ns)], axis=0)[:, :1]

    def hidden_copy(p, a):
        return pltpu.make_async_remote_copy(
            src_ref=hidden_all.at[s, p],
            dst_ref=hidden_all.at[s, p],
            send_sem=hidden_send.at[p, a],
            recv_sem=hidden_recv.at[p, s],
            device_id=peer(a, 0),
            device_id_type=MESH,
        )

    def hidden_arrive(p, a):
        source = lax.rem(s + a, ns)
        return pltpu.make_async_remote_copy(
            src_ref=hidden_all.at[s, p],
            dst_ref=hidden_all.at[source, p],
            send_sem=hidden_send.at[p, a],
            recv_sem=hidden_recv.at[p, source],
            device_id=peer(a, 0),
            device_id_type=MESH,
        )

    for copy in weight_copies[1]:
        copy.wait()
    for p in range(parts):
        at = slice(2 * p * span, 2 * (p + 1) * span)
        product = total_in[:, at]
        for source in range(nx):
            product = product + product_of(1, source, chunks[source], at)
        product = product * scale
        hidden_all[s, p] = (jax.nn.silu(product[:, :span]) * product[:, span:]).astype(BF16)
        for a in range(1, ns):
            hidden_copy(p, a).start()

    probs = [jax.nn.sigmoid(added[i : i + 1, :] * inverse) for i in range(2)]
    gates = [r / (probs[0] + probs[1]) for r in probs]
    weighted = jnp.concatenate(
        [
            place[e]
            * (
                jnp.where(id_rows[0] == e, gates[0], 0.0)
                + jnp.where(id_rows[1] == e, gates[1], 0.0)
            )
            for e in range(nx)
        ],
        axis=0,
    )
    slots = nx * CAP
    padded[...] = jnp.zeros_like(padded)
    padded[:slots, :] = weighted
    weighted = padded[...].T[:, :slots]
    weighted_high = weighted.astype(BF16)
    weighted_low = (weighted - weighted_high.astype(F32)).astype(BF16)

    def down_product(p, at):
        hidden = jnp.concatenate([hidden_all[i, p] for i in range(ns)], axis=1)
        return jnp.dot(
            hidden,
            weights_down[p, :, :, at].reshape(ns * span, -1),
            preferred_element_type=F32,
        )

    def back_copy(h, block):
        return pltpu.make_async_remote_copy(
            src_ref=back_out.at[h, block],
            dst_ref=back_in.at[h, x],
            send_sem=back_send.at[h, block],
            recv_sem=back_recv.at[h, x],
            device_id={"seq": block, "exp": s},
            device_id_type=MESH,
        )

    def back_arrive(h, e):
        return pltpu.make_async_remote_copy(
            src_ref=back_out.at[h, 0],
            dst_ref=back_in.at[h, e],
            send_sem=back_send.at[h, 0],
            recv_sem=back_recv.at[h, e],
            device_id={"seq": x, "exp": e},
            device_id_type=MESH,
        )

    for p in range(parts):
        for a in range(1, ns):
            hidden_arrive(p, a).wait_recv()
        for copy in down_copies[p]:
            copy.wait()
        if p < parts - 1:
            product = down_product(p, slice(0, width))
            total_out[...] = product if p == 0 else total_out[...] + product
    for h in range(2):
        at = slice(h * half, (h + 1) * half)
        total = down_product(parts - 1, at)
        if parts > 1:
            total = total + total_out[:, at]
        for b in range(ns):
            of = slice(b * CAP, (b + 1) * CAP)
            back_out[h, b] = jnp.concatenate(
                [total[of, :quarter], total[of, quarter:]], axis=0
            ).astype(BF16)
        for a in range(1, ns):
            back_copy(h, lax.rem(s + a, ns)).start()

        @pl.when(x != s)
        def _():
            back_copy(h, s).start()

        @pl.when(x == s)
        def _():
            back_in[h, x] = back_out[h, s]

    def out_copy(h):
        at = pl.ds(h * half, half)
        return pltpu.make_async_copy(out.at[:, at], out_hbm.at[:, at], out_sems.at[h])

    for h in range(2):
        for b in range(1, nx):
            back_arrive(h, lax.rem(x + b, nx)).wait_recv()

        @pl.when(x != s)
        def _():
            back_arrive(h, x).wait_recv()

        returned = [back_in[h, e].astype(F32) for e in range(nx)]
        expert_out = jnp.concatenate(
            [
                jnp.concatenate([r[j * CAP : (j + 1) * CAP] for r in returned], axis=0)
                for j in range(2)
            ],
            axis=1,
        ).astype(BF16)
        combined = jnp.dot(weighted_high, expert_out, preferred_element_type=F32) + jnp.dot(
            weighted_low, expert_out, preferred_element_type=F32
        )
        at = slice(h * half, (h + 1) * half)
        out[:, at] = (mixed[:, at].astype(F32) + combined).astype(BF16)
        out_copy(h).start()

    for h in range(2):
        out_copy(h).wait()

    @pl.when(s < ns - 1)
    def _():
        for head in range(heads):
            chain_copy(head).wait_send()

    for m in range(2):
        for a, b in peers:
            slots_copy(m, a, b).wait_send()
    for b in range(1, nx):
        sums_copy(b).wait_send()
    for a in range(1, ns):
        inverse_copy(a).wait_send()
        for p in range(parts):
            hidden_copy(p, a).wait_send()
    for h in range(2):
        for a in range(1, ns):
            back_copy(h, lax.rem(s + a, ns)).wait_send()

        @pl.when(x != s)
        def _():
            back_copy(h, s).wait_send()


def fused_body(
    residual,
    query_rows,
    key_rows,
    value_rows,
    log_decay,
    attn_gain,
    norm_gain,
    router,
    expert_ids,
    priority,
    gate_weight,
    up_weight,
    down_weight,
):
    ns, nx = lax.axis_size("seq"), lax.axis_size("exp")
    rows, width = residual.shape
    heads = width // HEAD
    group = 2 if heads % 4 == 0 else 1
    depth, ff = gate_weight.shape[1:]
    half = width // 2
    parts = next(n for n in (3, 2, 1) if ff % (n * HEAD) == 0)
    dma = pltpu.SemaphoreType.DMA
    inputs = (
        residual,
        query_rows,
        key_rows,
        value_rows,
        log_decay.T,
        attn_gain.reshape(heads, HEAD),
        norm_gain.reshape(heads, HEAD),
        router.T,
        expert_ids.T,
        priority,
    )
    in_place = pl.BlockSpec(memory_space=pl.ANY)
    return pl.pallas_call(
        functools.partial(layer_kernel, ns, nx, group, parts),
        out_shape=jax.ShapeDtypeStruct((rows, width), BF16),
        in_specs=[in_place] * (INPUTS + 3),
        out_specs=in_place,
        scratch_shapes=[pltpu.VMEM(a.shape, a.dtype) for a in inputs]
        + [
            pltpu.VMEM((rows, width), BF16),
            dma((INPUTS,)),
            dma((2,)),
            pltpu.VMEM((nx, 2, half, 2 * ff), BF16),
            pltpu.VMEM((parts, ns, ff // parts, width), BF16),
            pltpu.VMEM((rows, rows), F32),
            pltpu.VMEM((rows, rows), F32),
            pltpu.VMEM((rows, width), BF16),
            pltpu.VMEM((heads, HEAD, HEAD), F32),
            pltpu.VMEM((heads, HEAD, HEAD), BF16),
            pltpu.VMEM((heads, HEAD, HEAD), BF16),
            pltpu.VMEM((8, rows), F32),
            pltpu.VMEM((nx, 8, rows), F32),
            pltpu.VMEM((2, nx, 2 * CAP, half // 2), BF16),
            pltpu.VMEM((2, ns, nx, 2 * CAP, half // 2), BF16),
            pltpu.VMEM((nx, CAP, rows), F32),
            pltpu.VMEM((ns, CAP, rows), F32),
            pltpu.VMEM((ns * CAP, 2 * ff), F32),
            pltpu.VMEM((ns, parts, ns * CAP, ff // parts), BF16),
            pltpu.VMEM((ns * CAP, width), F32),
            pltpu.VMEM((2, ns, 2 * CAP, half // 2), BF16),
            pltpu.VMEM((2, nx, 2 * CAP, half // 2), BF16),
            pltpu.VMEM((nx, ns * CAP, half), BF16),
            dma((2, parts, 2)),
            dma((parts,)),
            dma((2, heads)),
            dma((nx,)),
            dma((nx,)),
            dma((2, ns, nx)),
            dma((2, ns, nx)),
            dma((ns,)),
            dma((ns,)),
            dma((parts, ns)),
            dma((parts, ns)),
            dma((2, ns)),
            dma((2, nx)),
        ],
        compiler_params=pltpu.CompilerParams(
            collective_id=0, has_side_effects=True, vmem_limit_bytes=60 * 1024 * 1024
        ),
        cost_estimate=pl.CostEstimate(
            flops=6 * ns * CAP * depth * ff,
            bytes_accessed=6 * depth * ff,
            transcendentals=heads * rows * rows,
        ),
    )(
        *inputs,
        gate_weight.reshape(nx, 2, half, ff),
        up_weight.reshape(nx, 2, half, ff),
        down_weight.reshape(ns, parts, ff // parts, width),
    )


def body(*args):
    rows, width = args[0].shape
    ff, columns = args[10].shape[2], args[12].shape[2]
    aligned = (
        rows == HEAD
        and ff % HEAD == 0
        and width % (4 * HEAD) == 0
        and columns == width
        and args[10].shape[0] == 1
        and lax.axis_size("seq") == lax.axis_size("exp")
    )
    return (fused_body if aligned else plain_body)(*args)


def solution(mesh):
    return jax.shard_map(
        body,
        mesh=mesh,
        in_specs=(
            P(("groups", "seq"), "exp"),
            P(("groups", "seq"), "exp"),
            P(("groups", "seq"), "exp"),
            P(("groups", "seq"), "exp"),
            P(("groups", "seq"), "exp"),
            P("exp"),
            P("exp"),
            P("exp", None),
            P(("groups", "seq"), None),
            P(("groups", "seq"), None),
            P("exp", None, "seq"),
            P("exp", None, "seq"),
            P("exp", None, "seq"),
        ),
        out_specs=P(("groups", "seq"), "exp"),
        check_vma=False,
    )
```

```python
import functools

import jax
import jax.numpy as jnp
from jax import lax
from jax.experimental import pallas as pl
from jax.experimental.pallas import tpu as pltpu
from jax.sharding import PartitionSpec as P

D = 6144
HEAD = 128
EXPERTS = 32
CAP = 8


def link_states(earlier, later):
    return (earlier[0] * later[0], later[0] * earlier[1] + later[1])


def plain_body(
    residual,
    query_rows,
    key_rows,
    value_rows,
    log_decay,
    attn_gain,
    norm_gain,
    router,
    expert_ids,
    priority,
    gate_weight,
    up_weight,
    down_weight,
):
    rows = residual.shape[0]
    width = residual.shape[1]
    heads = width // HEAD
    held = lax.axis_size("exp")
    queries = query_rows.reshape(rows, heads, HEAD)
    keys_local = key_rows.reshape(rows, heads, HEAD)
    values = value_rows.reshape(rows, heads, HEAD)
    cumulative = jnp.cumsum(log_decay, axis=0)
    scores = jnp.einsum("thd,shd->hts", queries, keys_local, preferred_element_type=jnp.float32)
    causal = (jnp.arange(rows)[:, None] >= jnp.arange(rows)[None, :])[None]
    spread = cumulative.T[:, :, None] - cumulative.T[:, None, :]
    weights = jnp.where(causal, scores * jnp.exp(jnp.where(causal, spread, 0.0)), 0.0).astype(
        jnp.bfloat16
    )
    local_part = jnp.einsum("hts,shd->thd", weights, values, preferred_element_type=jnp.float32)
    to_end = jnp.exp(cumulative[-1][None, :] - cumulative)
    keyed = (keys_local.astype(jnp.float32) * to_end[:, :, None]).astype(jnp.bfloat16)
    block_state = jnp.einsum("thd,the->hde", keyed, values, preferred_element_type=jnp.float32)
    block_decay = jnp.exp(cumulative[-1])
    seq_count = lax.axis_size("seq")
    share_size = block_state.size // seq_count
    flat_state = block_state.reshape(seq_count, share_size)
    tiled_decay = jnp.broadcast_to(block_decay[None, :], (seq_count, heads))
    arrived_state, arrived_decay = (
        lax.all_to_all(flat_state, "seq", split_axis=0, concat_axis=0, tiled=True),
        lax.all_to_all(tiled_decay, "seq", split_axis=0, concat_axis=0, tiled=True),
    )
    position = lax.axis_index("seq") * share_size + jnp.arange(share_size, dtype=jnp.int32)
    owner_head = position // (HEAD * HEAD)
    selector = jnp.where(
        owner_head[None, :] == jnp.arange(heads, dtype=jnp.int32)[:, None], 1.0, 0.0
    ).astype(jnp.float32)
    element_decay = jnp.dot(arrived_decay, selector, precision=lax.Precision.HIGHEST)
    inclusive = lax.associative_scan(link_states, (element_decay, arrived_state), axis=0)[1]
    exclusive = jnp.concatenate([jnp.zeros((1, share_size), jnp.float32), inclusive[:-1]], axis=0)
    returned_prefix = lax.all_to_all(exclusive, "seq", split_axis=0, concat_axis=0, tiled=True)
    prior_state = returned_prefix.reshape(block_state.shape)
    inter = jnp.einsum(
        "thd,hde->the", queries.astype(jnp.float32), prior_state, precision=lax.Precision.HIGHEST
    )
    attended = local_part + jnp.exp(cumulative)[:, :, None] * inter
    normed = attended * lax.rsqrt(jnp.mean(attended * attended, axis=-1, keepdims=True) + 1e-06)
    normed = normed * attn_gain.reshape(heads, HEAD)
    mixed = (residual.astype(jnp.float32) + normed.reshape(rows, width)).astype(jnp.bfloat16)
    mixed_f = mixed.astype(jnp.float32)
    gained = mixed_f * norm_gain
    router_f = router.astype(jnp.float32)
    squares = lax.psum(jnp.sum(mixed_f * mixed_f, axis=1), "exp")
    inverse = lax.rsqrt(squares / D + 1e-06)
    scaled = gained * inverse[:, None]
    logits = lax.psum(jnp.dot(scaled, router_f, precision=lax.Precision.HIGHEST), "exp")
    tokens_in = scaled.astype(jnp.bfloat16)
    probs = jax.nn.sigmoid(logits)
    chosen = expert_ids[:, :, None] == jnp.arange(EXPERTS, dtype=jnp.int32)[None, None, :]
    selected = jnp.sum(jnp.where(chosen, probs[:, None, :], 0.0), axis=-1)
    gates = selected / jnp.sum(selected, axis=-1, keepdims=True)
    is_held = expert_ids[:, :, None] == jnp.arange(held, dtype=jnp.int32)[None, None, :]
    member = jnp.where(jnp.any(is_held, axis=1), 1.0, 0.0).astype(jnp.float32)
    gate_held = jnp.sum(jnp.where(is_held, gates[:, :, None], 0.0), axis=1)
    order = priority[0]
    earlier = jnp.where(order[None, :] < order[:, None], 1.0, 0.0).astype(jnp.bfloat16)
    rank = jnp.dot(earlier, member.astype(jnp.bfloat16), preferred_element_type=jnp.float32)
    kept = (member > 0.5) & (rank < CAP)
    slot_ids = jnp.arange(CAP).astype(jnp.float32)
    place = kept.T[:, None, :] & (rank.T[:, None, :] == slot_ids[None, :, None])
    place_f = jnp.where(place, 1.0, 0.0).astype(jnp.float32)
    buffer = jnp.einsum(
        "ect,td->ecd", place_f.astype(jnp.bfloat16), tokens_in, preferred_element_type=jnp.float32
    ).astype(jnp.bfloat16)
    arrived = lax.all_to_all(buffer, "exp", split_axis=0, concat_axis=2, tiled=True)[0]
    gathered = lax.all_gather(arrived, "seq", axis=0, tiled=True)
    gate = jnp.dot(gathered, gate_weight[0], preferred_element_type=jnp.float32)
    up = jnp.dot(gathered, up_weight[0], preferred_element_type=jnp.float32)
    hidden = (jax.nn.silu(gate) * up).astype(jnp.bfloat16)
    weight_rows = down_weight[0]
    summed = jnp.dot(
        lax.all_gather(hidden, "seq", axis=1, tiled=True),
        weight_rows,
        preferred_element_type=jnp.float32,
    )
    expert_out = summed.astype(jnp.bfloat16)
    returned = lax.all_to_all(expert_out, "seq", split_axis=0, concat_axis=1, tiled=True)
    regrouped = lax.all_to_all(returned[None], "exp", split_axis=2, concat_axis=0, tiled=True)
    weighted = place_f * gate_held.T[:, None, :]
    combined = jnp.einsum(
        "ect,ecd->td", weighted, regrouped.astype(jnp.float32), precision=lax.Precision.HIGHEST
    )
    return (mixed_f + combined).astype(jnp.bfloat16)


MESH = pl.DeviceIdType.MESH
F32 = jnp.float32
INPUTS = 10
BF16 = jnp.bfloat16


def layer_kernel(
    ns,
    nx,
    group,
    parts,
    *refs,
):
    arrays, refs = refs[:INPUTS], refs[INPUTS:]
    (gate_hbm, up_hbm, down_hbm, out_hbm), refs = refs[:4], refs[4:]
    local, refs = refs[:INPUTS], refs[INPUTS:]
    (residual, query, key, value, log_decay, attn_gain, norm_gain, router, ids, priority) = local
    (
    out,
    input_sems,
    out_sems,
    weights_in,
    weights_down,
    padded,
    cum_rows,
    mixed,
    states,
    nearby,
    chain_out,
    chain_in,
    sums_out,
    sums_in,
    slots_out,
    slots_in,
    inverse_out,
    inverse_in,
    total_in,
    hidden_all,
    total_out,
    back_out,
    back_in,
    chunks,
    weight_sems,
    down_sems,
    chain_sems,
    sums_send,
    sums_recv,
    slots_send,
    slots_recv,
    inverse_send,
    inverse_recv,
    hidden_send,
    hidden_recv,
    back_send,
    back_recv,
    ) = refs
    rows, width = residual.shape
    heads = width // HEAD
    half = width // 2
    ff = gate_hbm.shape[3]
    span = ff // parts
    s = lax.axis_index("seq")
    x = lax.axis_index("exp")

    barrier = pltpu.get_barrier_semaphore()
    peers = [(a, b) for a in range(ns) for b in range(nx) if (a, b) != (0, 0)]

    def peer(a, b):
        return {"seq": lax.rem(s + a, ns), "exp": lax.rem(x + b, nx)}

    for a, b in peers:
        pl.semaphore_signal(barrier, inc=1, device_id=peer(a, b), device_id_type=MESH)

    input_copies = {}
    for i in (4, 8, 9, 2, 3, 1, 0, 5, 6, 7):
        input_copies[i] = pltpu.make_async_copy(arrays[i], local[i], input_sems.at[i])
        input_copies[i].start()

    def ready(*which):
        for i in which:
            input_copies[i].wait()

    weight_copies = [
        [
            pltpu.make_async_copy(
                source.at[:, m, :, pl.ds(p * span, span)],
                weights_in.at[:, m, :, pl.ds((2 * p + j) * span, span)],
                weight_sems.at[m, p, j],
            )
            for p in range(parts)
            for j, source in enumerate((gate_hbm, up_hbm))
        ]
        for m in range(2)
    ]
    down_copies = [
        [pltpu.make_async_copy(down_hbm.at[:, p], weights_down.at[p], down_sems.at[p])]
        for p in range(parts)
    ]
    for copies in weight_copies + down_copies:
        for copy in copies:
            copy.start()

    ready(4, 8, 9)
    row_at = lax.broadcasted_iota(jnp.int32, (rows, rows), 0)
    lane_at = lax.broadcasted_iota(jnp.int32, (rows, rows), 1)
    id_rows = [ids[i : i + 1, :].astype(F32) for i in range(2)]
    order = jnp.broadcast_to(priority[...].astype(F32), (rows, rows))
    earlier = jnp.where(order.T < order, 1.0, 0.0).astype(BF16)
    expert_rows = -(-nx // 8) * 8
    expert_at = lax.broadcasted_iota(jnp.int32, (expert_rows, rows), 0).astype(F32)
    member = jnp.where((id_rows[0] == expert_at) | (id_rows[1] == expert_at), 1.0, 0.0)
    rank = jnp.dot(member.astype(BF16), earlier, preferred_element_type=F32)
    slot_at = lax.broadcasted_iota(jnp.int32, (CAP, rows), 0).astype(F32)
    rank = jnp.where(member > 0.5, rank, -1.0)
    place = [jnp.where(rank[e : e + 1, :] == slot_at, 1.0, 0.0) for e in range(nx)]
    place_all = jnp.concatenate(place, axis=0)

    padded[...] = jnp.zeros_like(padded)
    padded[:heads, :] = log_decay[...]
    upper = jnp.where(row_at <= lane_at, 1.0, 0.0).astype(F32)
    cumulative = jnp.dot(
        padded[...], upper, precision=lax.Precision.HIGHEST, preferred_element_type=F32
    )
    cum_rows[...] = cumulative
    padded[...] = cumulative.T

    @pl.when(s == 0)
    def _():
        chain_in[...] = jnp.zeros_like(chain_in)

    pl.semaphore_wait(barrier, len(peers))

    def chain_copy(i):
        return pltpu.make_async_remote_copy(
            src_ref=chain_out.at[i],
            dst_ref=chain_in.at[i],
            send_sem=chain_sems.at[0, i],
            recv_sem=chain_sems.at[1, i],
            device_id={"seq": lax.rem(s + 1, ns)},
            device_id_type=MESH,
        )

    ready(2, 3)
    cluster = 2 * group
    for first in range(0, heads, cluster):
        for head in range(first, first + cluster):
            at = slice(head * HEAD, (head + 1) * HEAD)
            col = padded[:, head : head + 1]
            to_end = jnp.exp(col[rows - 1 : rows, :] - col)
            keyed = (key[:, at].astype(F32) * to_end).astype(BF16)
            state = lax.dot_general(
                keyed, value[:, at], (((0,), (0,)), ((), ())), preferred_element_type=F32
            )
            states[head] = state
            chain_out[head] = state.astype(BF16)

        @pl.when(s == 0)
        def _():
            for head in range(first, first + cluster):
                chain_copy(head).start()

    ready(0, 1, 5, 6, 7)
    causal = row_at >= lane_at
    for head in range(heads):
        at = slice(head * HEAD, (head + 1) * HEAD)
        spread = jnp.where(causal, padded[:, head : head + 1] - cum_rows[head : head + 1, :], 0.0)
        scores = lax.dot_general(
            query[:, at], key[:, at], (((1,), (1,)), ((), ())), preferred_element_type=F32
        )
        weights = jnp.where(causal, scores * jnp.exp(spread), 0.0).astype(BF16)
        nearby[:, at] = jnp.dot(weights, value[:, at], preferred_element_type=F32)

    def attend(first):
        these = range(first, first + group)

        @pl.when(s > 0)
        def _():
            for head in these:
                chain_copy(head).wait_recv()

                @pl.when(s < ns - 1)
                def _():
                    decay = jnp.exp(padded[rows - 1 : rows, head : head + 1])
                    prior = chain_in[head].astype(F32)
                    chain_out[head] = (decay * prior + states[head]).astype(BF16)
                    chain_copy(head).start()

        for head in these:
            at = slice(head * HEAD, (head + 1) * HEAD)
            inter = jnp.dot(query[:, at], chain_in[head], preferred_element_type=F32)
            attended = nearby[:, at] + jnp.exp(padded[:, head : head + 1]) * inter
            mean = jnp.sum(attended * attended, axis=1, keepdims=True) / HEAD
            normed = attended * lax.rsqrt(mean + 1e-06) * attn_gain[head : head + 1, :]
            mixed[:, at] = (residual[:, at].astype(F32) + normed).astype(BF16)

    def slots_copy(m, a, b):
        return pltpu.make_async_remote_copy(
            src_ref=slots_out.at[m, lax.rem(x + b, nx)],
            dst_ref=slots_in.at[m, s, x],
            send_sem=slots_send.at[m, a, b],
            recv_sem=slots_recv.at[m, s, x],
            device_id=peer(a, b),
            device_id_type=MESH,
        )

    def slots_arrive(m, block, source):
        return pltpu.make_async_remote_copy(
            src_ref=slots_out.at[m, 0],
            dst_ref=slots_in.at[m, block, source],
            send_sem=slots_send.at[m, 0, 0],
            recv_sem=slots_recv.at[m, block, source],
            device_id=peer(1, 1),
            device_id_type=MESH,
        )

    place_b = place_all.astype(BF16)
    heads_half = heads // 2
    quarter = half // 2
    logits = jnp.zeros((rows, router.shape[0]), F32)
    squares = jnp.zeros((rows, 1), F32)
    for m in range(2):
        for first in range(m * heads_half, (m + 1) * heads_half, group):
            attend(first)
        gained = []
        for head in range(m * heads_half, (m + 1) * heads_half):
            mixed_f = mixed[:, head * HEAD : (head + 1) * HEAD].astype(F32)
            squares = squares + jnp.sum(mixed_f * mixed_f, axis=1, keepdims=True)
            gained.append(mixed_f * norm_gain[head : head + 1, :])
        gained = jnp.concatenate(gained, axis=1)
        tokens = gained.astype(BF16)
        picked = jnp.dot(place_b, tokens, preferred_element_type=F32)
        for e in range(nx):
            at = slice(e * CAP, (e + 1) * CAP)
            slots_out[m, e] = jnp.concatenate(
                [picked[at, :quarter], picked[at, quarter:]], axis=0
            ).astype(BF16)
        slots_in[m, s, x] = slots_out[m, x]
        for a, b in peers:
            slots_copy(m, a, b).start()
        rest = (gained - tokens.astype(F32)).astype(BF16)
        router_half = router[:, m * half : (m + 1) * half]
        for part in (tokens, rest):
            logits = logits + lax.dot_general(
                part, router_half, (((1,), (1,)), ((), ())), preferred_element_type=F32
            )

    padded[...] = jnp.zeros_like(padded)
    padded[:, : router.shape[0]] = logits
    logits_t = padded[...].T
    expert_row = row_at.astype(F32)
    chosen = [
        jnp.sum(jnp.where(expert_row == r, logits_t, 0.0), axis=0, keepdims=True) for r in id_rows
    ]
    squares_t = jnp.broadcast_to(squares, (rows, rows)).T[0:1, :]
    sums = jnp.concatenate([chosen[0], chosen[1], squares_t] + [squares_t] * 5, axis=0)
    sums_out[...] = sums
    sums_in[x] = sums

    def sums_copy(b):
        return pltpu.make_async_remote_copy(
            src_ref=sums_out,
            dst_ref=sums_in.at[x],
            send_sem=sums_send.at[b],
            recv_sem=sums_recv.at[x],
            device_id=peer(0, b),
            device_id_type=MESH,
        )

    def sums_arrive(b):
        source = lax.rem(x + b, nx)
        return pltpu.make_async_remote_copy(
            src_ref=sums_out,
            dst_ref=sums_in.at[source],
            send_sem=sums_send.at[b],
            recv_sem=sums_recv.at[source],
            device_id=peer(0, b),
            device_id_type=MESH,
        )

    for b in range(1, nx):
        sums_copy(b).start()

    def slots_wait(m):
        for a, b in peers:
            slots_arrive(m, lax.rem(s + a, ns), lax.rem(x + b, nx)).wait_recv()

    def chunk_of(m, source):
        arrived = [slots_in[m, i, source].astype(F32) for i in range(ns)]
        return jnp.concatenate(
            [
                jnp.concatenate([r[h * CAP : (h + 1) * CAP] for r in arrived], axis=0)
                for h in range(2)
            ],
            axis=1,
        ).astype(BF16)

    def product_of(m, source, chunk, at):
        return jnp.dot(chunk, weights_in[source, m, :, at], preferred_element_type=F32)

    slots_wait(0)
    for copy in weight_copies[0]:
        copy.wait()
    for source in range(nx):
        product = product_of(0, source, chunk_of(0, source), slice(0, 2 * ff))
        total_in[...] = product if source == 0 else total_in[...] + product

    for b in range(1, nx):
        sums_arrive(b).wait_recv()
    added = sums_in[0]
    for b in range(1, nx):
        added = added + sums_in[b]
    inverse = lax.rsqrt(added[2:3, :] / (width * nx) + 1e-06)
    slot_inverse = jnp.sum(place_all * inverse, axis=1, keepdims=True)
    slot_inverse = jnp.broadcast_to(slot_inverse, place_all.shape)
    for e in range(nx):
        inverse_out[e] = slot_inverse[e * CAP : (e + 1) * CAP, :]
    inverse_in[s] = inverse_out[x]

    def inverse_copy(a):
        return pltpu.make_async_remote_copy(
            src_ref=inverse_out.at[x],
            dst_ref=inverse_in.at[s],
            send_sem=inverse_send.at[a],
            recv_sem=inverse_recv.at[s],
            device_id=peer(a, 0),
            device_id_type=MESH,
        )

    def inverse_arrive(a):
        source = lax.rem(s + a, ns)
        return pltpu.make_async_remote_copy(
            src_ref=inverse_out.at[x],
            dst_ref=inverse_in.at[source],
            send_sem=inverse_send.at[a],
            recv_sem=inverse_recv.at[source],
            device_id=peer(a, 0),
            device_id_type=MESH,
        )

    for a in range(1, ns):
        inverse_copy(a).start()

    slots_wait(1)
    for source in range(nx):
        chunks[source] = chunk_of(1, source)
    for a in range(1, ns):
        inverse_arrive(a).wait_recv()
    scale = jnp.concatenate([inverse_in[i] for i in range(ns)], axis=0)[:, :1]

    def hidden_copy(p, a):
        return pltpu.make_async_remote_copy(
            src_ref=hidden_all.at[s, p],
            dst_ref=hidden_all.at[s, p],
            send_sem=hidden_send.at[p, a],
            recv_sem=hidden_recv.at[p, s],
            device_id=peer(a, 0),
            device_id_type=MESH,
        )

    def hidden_arrive(p, a):
        source = lax.rem(s + a, ns)
        return pltpu.make_async_remote_copy(
            src_ref=hidden_all.at[s, p],
            dst_ref=hidden_all.at[source, p],
            send_sem=hidden_send.at[p, a],
            recv_sem=hidden_recv.at[p, source],
            device_id=peer(a, 0),
            device_id_type=MESH,
        )

    for copy in weight_copies[1]:
        copy.wait()
    for p in range(parts):
        at = slice(2 * p * span, 2 * (p + 1) * span)
        product = total_in[:, at]
        for source in range(nx):
            product = product + product_of(1, source, chunks[source], at)
        product = product * scale
        hidden_all[s, p] = (jax.nn.silu(product[:, :span]) * product[:, span:]).astype(BF16)
        for a in range(1, ns):
            hidden_copy(p, a).start()

    def down_product(p, at):
        hidden = jnp.concatenate([hidden_all[i, p] for i in range(ns)], axis=1)
        return jnp.dot(
            hidden,
            weights_down[p, :, :, at].reshape(ns * span, -1),
            preferred_element_type=F32,
        )

    def back_copy(h, block):
        return pltpu.make_async_remote_copy(
            src_ref=back_out.at[h, block],
            dst_ref=back_in.at[h, x],
            send_sem=back_send.at[h, block],
            recv_sem=back_recv.at[h, x],
            device_id={"seq": block, "exp": s},
            device_id_type=MESH,
        )

    def back_arrive(h, e):
        return pltpu.make_async_remote_copy(
            src_ref=back_out.at[h, 0],
            dst_ref=back_in.at[h, e],
            send_sem=back_send.at[h, 0],
            recv_sem=back_recv.at[h, e],
            device_id={"seq": x, "exp": e},
            device_id_type=MESH,
        )

    for p in range(parts):
        for a in range(1, ns):
            hidden_arrive(p, a).wait_recv()
        for copy in down_copies[p]:
            copy.wait()
        if p < parts - 1:
            product = down_product(p, slice(0, width))
            total_out[...] = product if p == 0 else total_out[...] + product
    for h in range(2):
        at = slice(h * half, (h + 1) * half)
        total = down_product(parts - 1, at)
        if parts > 1:
            total = total + total_out[:, at]
        for b in range(ns):
            of = slice(b * CAP, (b + 1) * CAP)
            back_out[h, b] = jnp.concatenate(
                [total[of, :quarter], total[of, quarter:]], axis=0
            ).astype(BF16)
        for a in range(1, ns):
            back_copy(h, lax.rem(s + a, ns)).start()

        @pl.when(x != s)
        def _():
            back_copy(h, s).start()

        @pl.when(x == s)
        def _():
            back_in[h, x] = back_out[h, s]

    probs = [jax.nn.sigmoid(added[i : i + 1, :] * inverse) for i in range(2)]
    gates = [r / (probs[0] + probs[1]) for r in probs]
    weighted = jnp.concatenate(
        [
            place[e]
            * (
                jnp.where(id_rows[0] == e, gates[0], 0.0)
                + jnp.where(id_rows[1] == e, gates[1], 0.0)
            )
            for e in range(nx)
        ],
        axis=0,
    )
    slots = nx * CAP
    padded[...] = jnp.zeros_like(padded)
    padded[:slots, :] = weighted
    weighted = padded[...].T[:, :slots]
    weighted_high = weighted.astype(BF16)
    weighted_low = (weighted - weighted_high.astype(F32)).astype(BF16)

    def out_copy(h):
        at = pl.ds(h * half, half)
        return pltpu.make_async_copy(out.at[:, at], out_hbm.at[:, at], out_sems.at[h])

    for h in range(2):
        for b in range(1, nx):
            back_arrive(h, lax.rem(x + b, nx)).wait_recv()

        @pl.when(x != s)
        def _():
            back_arrive(h, x).wait_recv()

        returned = [back_in[h, e].astype(F32) for e in range(nx)]
        expert_out = jnp.concatenate(
            [
                jnp.concatenate([r[j * CAP : (j + 1) * CAP] for r in returned], axis=0)
                for j in range(2)
            ],
            axis=1,
        ).astype(BF16)
        combined = jnp.dot(weighted_high, expert_out, preferred_element_type=F32) + jnp.dot(
            weighted_low, expert_out, preferred_element_type=F32
        )
        at = slice(h * half, (h + 1) * half)
        out[:, at] = (mixed[:, at].astype(F32) + combined).astype(BF16)
        out_copy(h).start()

    for h in range(2):
        out_copy(h).wait()

    @pl.when(s < ns - 1)
    def _():
        for head in range(heads):
            chain_copy(head).wait_send()

    for m in range(2):
        for a, b in peers:
            slots_copy(m, a, b).wait_send()
    for b in range(1, nx):
        sums_copy(b).wait_send()
    for a in range(1, ns):
        inverse_copy(a).wait_send()
        for p in range(parts):
            hidden_copy(p, a).wait_send()
    for h in range(2):
        for a in range(1, ns):
            back_copy(h, lax.rem(s + a, ns)).wait_send()

        @pl.when(x != s)
        def _():
            back_copy(h, s).wait_send()


def fused_body(
    residual,
    query_rows,
    key_rows,
    value_rows,
    log_decay,
    attn_gain,
    norm_gain,
    router,
    expert_ids,
    priority,
    gate_weight,
    up_weight,
    down_weight,
):
    ns, nx = lax.axis_size("seq"), lax.axis_size("exp")
    rows, width = residual.shape
    heads = width // HEAD
    group = 2 if heads % 4 == 0 else 1
    depth, ff = gate_weight.shape[1:]
    half = width // 2
    parts = next(n for n in (3, 2, 1) if ff % (n * HEAD) == 0)
    dma = pltpu.SemaphoreType.DMA
    inputs = (
        residual,
        query_rows,
        key_rows,
        value_rows,
        log_decay.T,
        attn_gain.reshape(heads, HEAD),
        norm_gain.reshape(heads, HEAD),
        router.T,
        expert_ids.T,
        priority,
    )
    in_place = pl.BlockSpec(memory_space=pl.ANY)
    return pl.pallas_call(
        functools.partial(layer_kernel, ns, nx, group, parts),
        out_shape=jax.ShapeDtypeStruct((rows, width), BF16),
        in_specs=[in_place] * (INPUTS + 3),
        out_specs=in_place,
        scratch_shapes=[pltpu.VMEM(a.shape, a.dtype) for a in inputs]
        + [
            pltpu.VMEM((rows, width), BF16),
            dma((INPUTS,)),
            dma((2,)),
            pltpu.VMEM((nx, 2, half, 2 * ff), BF16),
            pltpu.VMEM((parts, ns, ff // parts, width), BF16),
            pltpu.VMEM((rows, rows), F32),
            pltpu.VMEM((rows, rows), F32),
            pltpu.VMEM((rows, width), BF16),
            pltpu.VMEM((heads, HEAD, HEAD), F32),
            pltpu.VMEM((rows, width), F32),
            pltpu.VMEM((heads, HEAD, HEAD), BF16),
            pltpu.VMEM((heads, HEAD, HEAD), BF16),
            pltpu.VMEM((8, rows), F32),
            pltpu.VMEM((nx, 8, rows), F32),
            pltpu.VMEM((2, nx, 2 * CAP, half // 2), BF16),
            pltpu.VMEM((2, ns, nx, 2 * CAP, half // 2), BF16),
            pltpu.VMEM((nx, CAP, rows), F32),
            pltpu.VMEM((ns, CAP, rows), F32),
            pltpu.VMEM((ns * CAP, 2 * ff), F32),
            pltpu.VMEM((ns, parts, ns * CAP, ff // parts), BF16),
            pltpu.VMEM((ns * CAP, width), F32),
            pltpu.VMEM((2, ns, 2 * CAP, half // 2), BF16),
            pltpu.VMEM((2, nx, 2 * CAP, half // 2), BF16),
            pltpu.VMEM((nx, ns * CAP, half), BF16),
            dma((2, parts, 2)),
            dma((parts,)),
            dma((2, heads)),
            dma((nx,)),
            dma((nx,)),
            dma((2, ns, nx)),
            dma((2, ns, nx)),
            dma((ns,)),
            dma((ns,)),
            dma((parts, ns)),
            dma((parts, ns)),
            dma((2, ns)),
            dma((2, nx)),
        ],
        compiler_params=pltpu.CompilerParams(
            collective_id=0, has_side_effects=True, vmem_limit_bytes=60 * 1024 * 1024
        ),
        cost_estimate=pl.CostEstimate(
            flops=6 * ns * CAP * depth * ff,
            bytes_accessed=6 * depth * ff,
            transcendentals=heads * rows * rows,
        ),
    )(
        *inputs,
        gate_weight.reshape(nx, 2, half, ff),
        up_weight.reshape(nx, 2, half, ff),
        down_weight.reshape(ns, parts, ff // parts, width),
    )


def body(*args):
    rows, width = args[0].shape
    ff, columns = args[10].shape[2], args[12].shape[2]
    aligned = (
        rows == HEAD
        and ff % HEAD == 0
        and width % (4 * HEAD) == 0
        and columns == width
        and args[10].shape[0] == 1
        and lax.axis_size("seq") == lax.axis_size("exp")
    )
    return (fused_body if aligned else plain_body)(*args)


def solution(mesh):
    return jax.shard_map(
        body,
        mesh=mesh,
        in_specs=(
            P(("groups", "seq"), "exp"),
            P(("groups", "seq"), "exp"),
            P(("groups", "seq"), "exp"),
            P(("groups", "seq"), "exp"),
            P(("groups", "seq"), "exp"),
            P("exp"),
            P("exp"),
            P("exp", None),
            P(("groups", "seq"), None),
            P(("groups", "seq"), None),
            P("exp", None, "seq"),
            P("exp", None, "seq"),
            P("exp", None, "seq"),
        ),
        out_specs=P(("groups", "seq"), "exp"),
        check_vma=False,
    )
```
